32 devices in a mesh: vrow: 4 (over z), img: 8 (over y, x, core).
Axes of the slice: x: 2, y: 2, z: 4, core: 2. Of those that a mesh axis runs over, the one named last changes fastest.
Arguments:
- features: bfloat16 [4, 16, 64, 512], P('vrow', None, 'img'), may hold values from -6 to 6
- weight_h: bfloat16 [64, 64, 3, 3], replicated, may hold values from -0.25 to 0.25
- weight_v: bfloat16 [64, 64, 3, 3], replicated, may hold values from -0.25 to 0.25
- beta_h: float32 [5, 64], replicated, may hold values from 0.2 to 1
- beta_v: float32 [5, 64], replicated, may hold values from 0.2 to 1
- shear_set: int32 [5], replicated, may hold values from -2 to 2
- cotangent: bfloat16 [8, 64, 4096], P('vrow', 'img'), may hold values from -6 to 6
Outputs:
- output: bfloat16 [8, 64, 4096], P('vrow', 'img')
- grad_features: bfloat16 [4, 16, 64, 512], P('vrow', None, 'img')
- grad_weight_h: float32 [64, 64, 3, 3], replicated
- grad_weight_v: float32 [64, 64, 3, 3], replicated
- grad_beta_h: float32 [5, 64], replicated
- grad_beta_v: float32 [5, 64], replicated
The draws below stay inside these ranges and needn't reach their ends.
All inputs are finite; a program needn't handle non-finite values.
Results may differ from the reference program's by a relative error of at most 0.0057.
Values may be sent and summed in bfloat16 or wider, within the bound.
A program may use at most 128 MiB of HBM per device.

```python
import jax
import jax.numpy as jnp
from jax import lax

C = 64
SHEARS = 5
SHIFT_MAX = 2
Y = 16
U = 4
V = 8
X = 64


def with_ends(values, key, least, top_value):
    extent = values.shape
    place = [jax.random.randint(jax.random.fold_in(key, axis), (), 0, extent[axis]) for axis in range(len(extent))]
    values = values.at[tuple(place)].set(least)
    longest = extent.index(max(extent))
    place[longest] = (place[longest] + 1) % extent[longest]
    return values.at[tuple(place)].set(top_value)


def steps_of(rng, shape, shards, smallest, high):
    factor_of, own = 1.0, jax.random.fold_in(rng, 6)
    for dim, parts in shards:
        steps = jnp.exp(jax.random.uniform(jax.random.fold_in(own, dim), (parts,), jnp.float32, smallest / len(shards), high / len(shards)))
        factor_of = factor_of * jnp.repeat(steps, shape[dim] // parts).reshape([-1 if axis == dim else 1 for axis in range(len(shape))])
    return factor_of


def gaussian(own_key, shape, scale, most, shards=(), held_as=jnp.bfloat16):
    factor_of = steps_of(own_key, shape, shards, -0.22, 0.18) if shards else 1.0
    values = jax.random.normal(own_key, shape, jnp.float32) * scale * factor_of
    return jnp.minimum(jnp.maximum(values, -most), most).astype(held_as)


def setup_inputs(seed: int = 0) -> dict:
    splits = jax.random.split(jax.random.key(seed), 8)
    features = gaussian(splits[0], (U, Y, X, V * C), 1.0, 6.0, ((0, 4), (2, 8)))
    weight_h = gaussian(splits[1], (C, C, 3, 3), (9 * C) ** -0.5, 0.25)
    weight_v = gaussian(splits[2], (C, C, 3, 3), (9 * C) ** -0.5, 0.25)
    beta_h = jnp.clip(jax.random.uniform(splits[3], (SHEARS, C), jnp.float32, 0.2, 1.0), 0.2, 1.0)
    beta_v = jnp.clip(jax.random.uniform(splits[4], (SHEARS, C), jnp.float32, 0.2, 1.0), 0.2, 1.0)
    shear_set = with_ends(jax.random.randint(splits[5], (SHEARS,), -SHIFT_MAX, SHIFT_MAX + 1), jax.random.fold_in(splits[5], 1), -SHIFT_MAX, SHIFT_MAX).astype(jnp.int32)
    cotangent = gaussian(splits[6], (V, X, U * Y * C), 1.0, 6.0, ((0, 4), (1, 8)))
    return {"features": features, "weight_h": weight_h, "weight_v": weight_v, "beta_h": beta_h, "beta_v": beta_v, "shear_set": shear_set, "cotangent": cotangent}


def shear(source, amounts):
    columns = source.shape[3]
    target = jnp.arange(columns, dtype=jnp.int32)[None, :] + amounts[:, None]
    inside = (target >= 0) & (target < columns)
    target = jnp.clip(target, 0, columns - 1).astype(jnp.int32)
    picked = jnp.take_along_axis(source, jnp.broadcast_to(target[None, None], source.shape), axis=3)
    return picked * inside[None, None].astype(source.dtype)


def conv_forward(source, kernel):
    return lax.conv_general_dilated(source.astype(jnp.float32), kernel.astype(jnp.float32), (1, 1), ((1, 1), (1, 1)), dimension_numbers=("NCHW", "OIHW", "NCHW"), precision=lax.Precision.HIGHEST)


def conv_inputs(grads, kernel):
    return lax.conv_general_dilated(grads.astype(jnp.float32), kernel.astype(jnp.float32)[:, :, ::-1, ::-1], (1, 1), ((1, 1), (1, 1)), dimension_numbers=("NCHW", "IOHW", "NCHW"), precision=lax.Precision.HIGHEST)


def conv_kernel(grads, source):
    result = lax.conv_general_dilated(source.astype(jnp.float32), grads.astype(jnp.float32), (1, 1), ((1, 1), (1, 1)), dimension_numbers=("CNHW", "IOHW", "NCHW"), precision=lax.Precision.HIGHEST)
    return jnp.transpose(result, (1, 0, 2, 3))


def offsets_of(count):
    return jnp.arange(count, dtype=jnp.int32) - count // 2


def epi_forward(source, kernel, blend, shear_set):
    offsets = offsets_of(source.shape[2])
    branch = jnp.zeros(source.shape, jnp.float32)
    for shear_idx in range(SHEARS):
        amounts = (shear_set[shear_idx] * offsets).astype(jnp.int32)
        sheared = shear(source, amounts)
        preact = conv_forward(sheared, kernel)
        branch = branch + blend[shear_idx][None, :, None, None] * shear(jax.nn.silu(preact), -amounts)
    return (source.astype(jnp.float32) + branch).astype(jnp.bfloat16)


def epi_backward(source, kernel, blend, shear_set, grads):
    offsets = offsets_of(source.shape[2])
    total = grads
    kernel_grad = jnp.zeros((C, C, 3, 3), jnp.float32)
    blend_rows = []
    for shear_idx in range(SHEARS):
        amounts = (shear_set[shear_idx] * offsets).astype(jnp.int32)
        sheared = shear(source, amounts)
        preact = conv_forward(sheared, kernel)
        blend_rows.append(jnp.sum(grads * shear(jax.nn.silu(preact), -amounts), axis=(0, 2, 3)))
        sigma = jax.nn.sigmoid(preact)
        slope = sigma * (1.0 + preact * (1.0 - sigma))
        dpre = (shear(blend[shear_idx][None, :, None, None] * grads, amounts) * slope).astype(jnp.bfloat16)
        kernel_grad = kernel_grad + conv_kernel(dpre, sheared)
        total = total + shear(conv_inputs(dpre, kernel), -amounts)
    return total.astype(jnp.bfloat16), kernel_grad, jnp.stack(blend_rows)


def reference(features, weight_h, weight_v, beta_h, beta_v, shear_set, cotangent):
    u_all, y_all, x_all, merged = features.shape
    channels = weight_h.shape[0]
    v_all = merged // channels
    layout = jnp.transpose(features.reshape(u_all, y_all, x_all, v_all, channels), (0, 1, 4, 3, 2))
    rows_flat = layout.reshape(u_all * y_all, channels, v_all, x_all)
    hfeat = epi_forward(rows_flat, weight_h, beta_h, shear_set)
    vert_in = jnp.transpose(hfeat.reshape(u_all, y_all, channels, v_all, x_all), (3, 4, 2, 0, 1)).reshape(v_all * x_all, channels, u_all, y_all)
    vout = epi_forward(vert_in, weight_v, beta_v, shear_set)
    output = jnp.transpose(vout.reshape(v_all, x_all, channels, u_all, y_all), (0, 1, 3, 4, 2)).reshape(v_all, x_all, u_all * y_all * channels)
    grad_v = jnp.transpose(cotangent.reshape(v_all, x_all, u_all, y_all, channels), (0, 1, 4, 2, 3)).reshape(v_all * x_all, channels, u_all, y_all).astype(jnp.float32)
    dvert, raw_weight_v, raw_beta_v = epi_backward(vert_in, weight_v, beta_v, shear_set, grad_v)
    grad_h = jnp.transpose(dvert.reshape(v_all, x_all, channels, u_all, y_all), (3, 4, 2, 0, 1)).reshape(u_all * y_all, channels, v_all, x_all).astype(jnp.float32)
    dhor, raw_weight_h, raw_beta_h = epi_backward(rows_flat, weight_h, beta_h, shear_set, grad_h)
    grad_features = jnp.transpose(dhor.reshape(u_all, y_all, channels, v_all, x_all), (0, 1, 4, 3, 2)).reshape(u_all, y_all, x_all, v_all * channels)
    factor = float(u_all * v_all * y_all * x_all) ** -0.5
    return output, grad_features, raw_weight_h * factor, raw_weight_v * factor, raw_beta_h * factor, raw_beta_v * factor
```

```python
import functools

import jax
import jax.numpy as jnp
from jax import lax
from jax.experimental import pallas as pl
from jax.experimental.pallas import tpu as pltpu
from jax.sharding import PartitionSpec as P

SHIFTS = (-2, -1, 0, 1, 2)
REACH = 3
TAPS = tuple((i, j) for i in (-1, 0, 1) for j in (-1, 0, 1))
LANES = 128
MESH = pl.DeviceIdType.MESH
VMEM_LIMIT = 60 * 1024 * 1024


def place_of(x, shift, shape, start):
    views = lax.broadcasted_iota(jnp.int32, shape, 0) - shape[0] // 2
    return start + x - shift * views


def tap_products(f_ref, w_ref, z_ref):
    _, nxe, nv2, s, _ = z_ref.shape
    nv = nv2 - 2
    zero = jnp.zeros((9, nxe, 1, s, LANES), jnp.float32)
    z_ref[:, :, 0:1] = zero
    z_ref[:, :, nv + 1 : nv + 2] = zero
    source = f_ref[...].reshape(nxe * nv * s, LANES)
    for t in range(0, 9, 2):
        last = min(t + 2, 9)
        got = jnp.dot(
            source, w_ref[:, t * LANES : last * LANES], preferred_element_type=jnp.float32
        )
        for k in range(t, last):
            part = got[:, (k - t) * LANES : (k - t + 1) * LANES]
            z_ref[k, :, 1 : nv + 1] = part.reshape(nxe, nv, s, LANES)


def preact_at(z_ref, x, index, shift, place, total):
    nv = z_ref.shape[2] - 2
    sums = {}
    for t, (i, j) in enumerate(TAPS):
        term = z_ref[t, x + (REACH + j + shift * i), 1 + i : 1 + i + nv]
        sums[j] = term if j not in sums else sums[j] + term
    low = jnp.where(place != 0, sums[-1], 0.0)
    high = jnp.where(place != total - 1, sums[1], 0.0)
    return sums[0] + low + high


def sigma_of(p):
    return 0.5 * jnp.tanh(0.5 * p) + 0.5


def store_dpre(d_ref, r_ref, x, index, place, total, keep, grad, blend, p, sigma):
    nv = grad.shape[0]
    act = jnp.where(keep, p * sigma, 0.0)
    r_ref[index] += jnp.sum(grad * act, axis=0)
    slope = sigma * (1.0 + p * (1.0 - sigma))
    dpre = jnp.where(keep, blend * grad * slope, 0.0)
    d_ref[0, index, x, 1 : nv + 1] = jnp.where(place != 0, dpre, 0.0)
    d_ref[1, index, x, 1 : nv + 1] = dpre
    d_ref[2, index, x, 1 : nv + 1] = jnp.where(place != total - 1, dpre, 0.0)


def clear_dpre(d_ref, r_ref, nx, pad):
    _, count, _, nv2, s, _ = d_ref.shape
    r_ref[...] = jnp.zeros_like(r_ref)
    for j in range(3):
        rim = jnp.zeros((count, pad, nv2, s, LANES), jnp.float32)
        d_ref[j, :, 0:pad] = rim
        d_ref[j, :, pad + nx : 2 * pad + nx] = rim
        side = jnp.zeros((count, nx, 1, s, LANES), jnp.float32)
        d_ref[j, :, pad : pad + nx, 0:1] = side
        d_ref[j, :, pad : pad + nx, nv2 - 1 : nv2] = side


def gather_dpre(d_ref, s_ref):
    nv2, s = d_ref.shape[3:5]
    nv = nv2 - 2

    def body(x, carry):
        for t, (i, j) in enumerate(TAPS):
            total = None
            for index, shift in enumerate(SHIFTS):
                term = d_ref[j + 1, index, x + (REACH - j - shift * i), 1 - i : 1 - i + nv]
                total = term if total is None else total + term
            s_ref[x, :, t * LANES : (t + 1) * LANES] = total.reshape(nv * s, LANES).astype(
                jnp.bfloat16
            )
        return carry

    lax.fori_loop(0, s_ref.shape[0], body, 0)


def pack_grads(source, stacked, r_ref, out_ref):
    wide = lax.dot_general(
        source, stacked, (((0,), (0,)), ((), ())), preferred_element_type=jnp.float32
    )
    half = LANES // 2
    first, second = wide[:half], wide[half:]
    left = lax.broadcasted_iota(jnp.int32, (half, LANES), 1) < half
    sums = jnp.sum(r_ref[...], axis=1)
    sums = sums + pltpu.roll(sums, half, 1)
    for m in range(5):
        low = slice(2 * m * LANES, (2 * m + 1) * LANES)
        even = first[:, low] + pltpu.roll(second[:, low], half, 1)
        if m < 4:
            high = slice((2 * m + 1) * LANES, (2 * m + 2) * LANES)
            odd = pltpu.roll(first[:, high], half, 1) + second[:, high]
        else:
            odd = jnp.concatenate(
                [sums, jnp.zeros((half - sums.shape[0], LANES), jnp.float32)], axis=0
            )
        out_ref[m] = jnp.where(left, even, odd)


def forward_kernel(total, start_ref, f_ref, w_ref, b_ref, h_ref, pre_ref, z_ref):
    nx, nvs, _ = h_ref.shape
    nv, s = pre_ref.shape[2:4]
    start = start_ref[0]
    tap_products(f_ref, w_ref, z_ref)

    def body(x, carry):
        out = f_ref[x + REACH].astype(jnp.float32).reshape(nv, s, LANES)
        for index, shift in enumerate(SHIFTS):
            place = place_of(x, shift, (nv, s, LANES), start)
            p = preact_at(z_ref, x, index, shift, place, total)
            pre_ref[index, x] = p
            keep = (place >= 0) & (place < total)
            out = out + b_ref[index : index + 1] * jnp.where(keep, p * sigma_of(p), 0.0)
        h_ref[x] = out.reshape(nvs, LANES).astype(jnp.bfloat16)
        return carry

    lax.fori_loop(0, nx, body, 0)


def both_kernel(
    nv, total, f_ref, w_ref, b_ref, g_ref, o_ref, e_ref, p_ref, z_ref, d_ref, r_ref, s_ref
):
    nx, nvs, _ = o_ref.shape
    s = nvs // nv
    tap_products(f_ref, w_ref, z_ref)
    clear_dpre(d_ref, r_ref, nx, REACH)

    def body(x, carry):
        out = f_ref[x + REACH].astype(jnp.float32).reshape(nv, s, LANES)
        grad = g_ref[x].astype(jnp.float32).reshape(nv, s, LANES)
        for index, shift in enumerate(SHIFTS):
            place = place_of(x, shift, (nv, s, LANES), 0)
            p = preact_at(z_ref, x, index, shift, place, total)
            sigma = sigma_of(p)
            keep = (place >= 0) & (place < total)
            blend = b_ref[index : index + 1]
            out = out + blend * jnp.where(keep, p * sigma, 0.0)
            store_dpre(
                d_ref, r_ref, x + REACH, index, place, total, keep, grad, blend, p, sigma
            )
        o_ref[x] = out.reshape(nvs, LANES).astype(jnp.bfloat16)
        return carry

    lax.fori_loop(0, nx, body, 0)
    gather_dpre(d_ref, s_ref)
    stacked = s_ref[...].reshape(nx * nvs, 9 * LANES)
    back = lax.dot_general(
        stacked, w_ref[...], (((1,), (1,)), ((), ())), preferred_element_type=jnp.float32
    )
    e_ref[...] = (g_ref[...].astype(jnp.float32) + back.reshape(nx, nvs, LANES)).astype(
        jnp.bfloat16
    )
    source = f_ref[REACH : REACH + nx].reshape(nx * nvs, LANES)
    pack_grads(source, stacked, r_ref, p_ref)


def backward_kernel(
    total,
    start_ref,
    f_ref,
    w_ref,
    b_ref,
    g_ref,
    pre_ref,
    e_ref,
    before_ref,
    after_ref,
    p_ref,
    d_ref,
    r_ref,
    s_ref,
):
    nx, nvs, _ = e_ref.shape
    nv, s = pre_ref.shape[2:4]
    start = start_ref[0]
    clear_dpre(d_ref, r_ref, nx, 2 * REACH)

    def body(x, carry):
        grad = g_ref[x].astype(jnp.float32).reshape(nv, s, LANES)
        for index, shift in enumerate(SHIFTS):
            place = place_of(x, shift, (nv, s, LANES), start)
            p = pre_ref[index, x]
            keep = (place >= 0) & (place < total)
            blend = b_ref[index : index + 1]
            store_dpre(
                d_ref,
                r_ref,
                x + 2 * REACH,
                index,
                place,
                total,
                keep,
                grad,
                blend,
                p,
                sigma_of(p),
            )
        return carry

    lax.fori_loop(0, nx, body, 0)
    gather_dpre(d_ref, s_ref)
    stacked = s_ref[...].reshape((nx + 2 * REACH) * nvs, 9 * LANES)
    back = lax.dot_general(
        stacked, w_ref[...], (((1,), (1,)), ((), ())), preferred_element_type=jnp.float32
    ).reshape(nx + 2 * REACH, nvs, LANES)
    before_ref[...] = back[:REACH].astype(jnp.bfloat16)
    after_ref[...] = back[nx + REACH :].astype(jnp.bfloat16)
    e_ref[...] = g_ref[...].astype(jnp.float32) + back[REACH : REACH + nx]
    source = f_ref[...].reshape((nx + 2 * REACH) * nvs, LANES)
    pack_grads(source, stacked, r_ref, p_ref)


def sum_kernel(
    rows, cols, x_ref, o_ref, part, heard, totals, send_a, recv_a, send_b, recv_b, send_c, recv_c
):
    row, col = lax.axis_index("vrow"), lax.axis_index("img")

    def at(r, c):
        return dict(device_id=(r, c), device_id_type=MESH)

    barrier = pltpu.get_barrier_semaphore()
    for k in range(1, cols):
        pl.semaphore_signal(barrier, inc=1, **at(row, lax.rem(col + k, cols)))
    for k in range(1, rows):
        pl.semaphore_signal(barrier, inc=1, **at(lax.rem(row + k, rows), col))
    pl.semaphore_wait(barrier, cols + rows - 2)

    sends = []
    for k in range(1, cols):
        to = lax.rem(col + k, cols)
        copy = pltpu.make_async_remote_copy(
            src_ref=x_ref.at[to],
            dst_ref=heard.at[k - 1],
            send_sem=send_a.at[k - 1],
            recv_sem=recv_a.at[k - 1],
            **at(row, to),
        )
        copy.start()
        sends.append(copy)
    total = x_ref[col]
    for k, copy in enumerate(sends):
        copy.wait_recv()
        total = total + heard[k]
    part[...] = total
    totals[row] = total
    more = []
    for k in range(1, rows):
        copy = pltpu.make_async_remote_copy(
            src_ref=part,
            dst_ref=totals.at[row],
            send_sem=send_b.at[k - 1],
            recv_sem=recv_b.at[k - 1],
            **at(lax.rem(row + k, rows), col),
        )
        copy.start()
        more.append(copy)
    for copy in more:
        copy.wait_recv()
    total = totals[0]
    for k in range(1, rows):
        total = total + totals[k]
    o_ref[col] = total
    last = []
    for k in range(1, cols):
        copy = pltpu.make_async_remote_copy(
            src_ref=o_ref.at[col],
            dst_ref=o_ref.at[col],
            send_sem=send_c.at[k - 1],
            recv_sem=recv_c.at[k - 1],
            **at(row, lax.rem(col + k, cols)),
        )
        copy.start()
        last.append(copy)
    for copy in last:
        copy.wait_recv()
    for copy in sends + more + last:
        copy.wait_send()


def sum_over_devices(x, rows, cols):
    count, depth, _ = x.shape
    shape = x.shape
    x = x.reshape(cols, count * depth // cols, LANES)
    chunk = x.shape[1:]
    dma = pltpu.SemaphoreType.DMA
    out = pl.pallas_call(
        functools.partial(sum_kernel, rows, cols),
        out_shape=jax.ShapeDtypeStruct(x.shape, jnp.float32),
        in_specs=[pl.BlockSpec(memory_space=pltpu.VMEM)],
        out_specs=pl.BlockSpec(memory_space=pltpu.VMEM),
        scratch_shapes=[
            pltpu.VMEM(chunk, jnp.float32),
            pltpu.VMEM((cols - 1,) + chunk, jnp.float32),
            pltpu.VMEM((rows,) + chunk, jnp.float32),
            dma((cols - 1,)),
            dma((cols - 1,)),
            dma((rows - 1,)),
            dma((rows - 1,)),
            dma((cols - 1,)),
            dma((cols - 1,)),
        ],
        compiler_params=pltpu.CompilerParams(
            collective_id=0, has_side_effects=True, vmem_limit_bytes=VMEM_LIMIT
        ),
        name="sum_over_devices",
    )(x)
    return out.reshape(shape)


def call(kernel, name, args, outs, scratch):
    whole = pl.BlockSpec(memory_space=pltpu.VMEM)
    specs = [
        pl.BlockSpec(memory_space=pltpu.SMEM) if arg.dtype == jnp.int32 else whole for arg in args
    ]
    return pl.pallas_call(
        kernel,
        out_shape=[jax.ShapeDtypeStruct(shape, dtype) for shape, dtype in outs],
        in_specs=specs,
        out_specs=[whole] * len(outs),
        scratch_shapes=[pltpu.VMEM(shape, dtype) for shape, dtype in scratch],
        compiler_params=pltpu.CompilerParams(vmem_limit_bytes=VMEM_LIMIT),
        name=name,
    )(*args)


def halo(leading, trailing, axis):
    count = lax.axis_size(axis)
    up = [(i, i + 1) for i in range(count - 1)]
    down = [(j, i) for i, j in up]
    return lax.ppermute(trailing, axis, up), lax.ppermute(leading, axis, down)


def per_device(features, weight_h, weight_v, beta_h, beta_v, shear_set, cotangent):
    rows, cols = lax.axis_size("vrow"), lax.axis_size("img")
    channels = weight_h.shape[0]
    u_local, y_all, x_local, merged = features.shape
    v_all = merged // channels
    v_local = v_all // rows
    u_all = u_local * rows
    x_all = x_local * cols
    s_h = u_local * y_all // 2
    s_v = v_local * x_local // 2
    f32, bf16 = jnp.float32, jnp.bfloat16
    count = len(SHIFTS)

    weights = jnp.stack([weight_h, weight_v]).reshape(2, channels, channels, 9)
    weights = jnp.transpose(weights, (0, 2, 3, 1))
    eye = jnp.eye(2, dtype=bf16)
    weights = weights[:, None, :, :, None, :] * eye[None, :, None, None, :, None]
    weights = weights.reshape(2, LANES, 9 * LANES)
    chosen = (jnp.asarray(SHIFTS, jnp.int32)[:, None] == shear_set[None, :]).astype(f32)
    betas = jnp.stack([beta_h, beta_v])
    blends = jnp.sum(chosen[None, :, :, None] * betas[:, None], axis=2)
    blends = jnp.tile(blends, (1, 1, 2))

    field = features.reshape(2, s_h, x_local, v_all, channels)
    field = jnp.transpose(field, (2, 3, 1, 0, 4)).reshape(x_local, v_all * s_h, LANES)
    before, after = halo(field[:REACH], field[x_local - REACH :], "img")
    wide = jnp.concatenate([before, field, after], axis=0)
    start = (lax.axis_index("img") * x_local).astype(jnp.int32).reshape(1)
    flat_h = (x_local, v_all * s_h, LANES)
    four_h = (v_all, s_h, LANES)
    hfeat, pre = call(
        functools.partial(forward_kernel, x_all),
        "forward_h",
        [start, wide, weights[0], blends[0]],
        [(flat_h, bf16), ((count, x_local) + four_h, f32)],
        [((9, x_local + 2 * REACH, v_all + 2) + four_h[1:], f32)],
    )

    block = hfeat.reshape(x_local, rows, v_local, s_h, 2, channels)
    block = jnp.transpose(block, (1, 4, 3, 2, 0, 5))
    block = block.reshape(rows, u_local, y_all, v_local * x_local * channels)
    moved = lax.all_to_all(block, "vrow", split_axis=0, concat_axis=0, tiled=True)
    vert = moved.reshape(u_all, y_all, 2, s_v, channels)
    flat_v = (y_all, u_all * s_v, LANES)
    vert = jnp.transpose(vert, (1, 0, 3, 2, 4)).reshape(flat_v)
    vert = jnp.pad(vert, ((REACH, REACH), (0, 0), (0, 0)))
    grad_v = cotangent.reshape(2, s_v, u_all, y_all, channels)
    grad_v = jnp.transpose(grad_v, (3, 2, 1, 0, 4)).reshape(flat_v)
    vout, dvert, packed_v = call(
        functools.partial(both_kernel, u_all, y_all),
        "both_v",
        [vert, weights[1], blends[1], grad_v],
        [(flat_v, bf16), (flat_v, bf16), ((5, channels, LANES), f32)],
        [
            ((9, y_all + 2 * REACH, u_all + 2, s_v, LANES), f32),
            ((3, count, y_all + 2 * REACH, u_all + 2, s_v, LANES), f32),
            ((count, s_v, LANES), f32),
            ((y_all, u_all * s_v, 9 * LANES), bf16),
        ],
    )
    output = jnp.transpose(vout.reshape(y_all, u_all, s_v, 2, channels), (3, 2, 1, 0, 4))
    output = output.reshape(v_local, x_local, u_all * y_all * channels)

    back = jnp.transpose(dvert.reshape(y_all, u_all, s_v, 2, channels), (1, 0, 3, 2, 4))
    back = back.reshape(rows, u_local, y_all, v_local * x_local * channels)
    returned = lax.all_to_all(back, "vrow", split_axis=0, concat_axis=0, tiled=True)
    returned = returned.reshape(rows, 2, s_h, v_local, x_local, channels)
    grad_h = jnp.transpose(returned, (4, 0, 3, 2, 1, 5)).reshape(flat_h)

    rim = (REACH, v_all * s_h, LANES)
    middle, to_before, to_after, packed_h = call(
        functools.partial(backward_kernel, x_all),
        "backward_h",
        [start, wide, weights[0], blends[0], grad_h, pre],
        [(flat_h, f32), (rim, bf16), (rim, bf16), ((5, channels, LANES), f32)],
        [
            ((3, count, x_local + 4 * REACH, v_all + 2) + four_h[1:], f32),
            ((count,) + four_h[1:], f32),
            ((x_local + 2 * REACH, v_all * s_h, 9 * LANES), bf16),
        ],
    )
    from_before, from_after = halo(to_before, to_after, "img")
    gap = ((0, x_local - REACH), (0, 0), (0, 0))
    middle = middle + jnp.pad(from_before, gap).astype(f32)
    middle = middle + jnp.pad(from_after, (gap[0][::-1], (0, 0), (0, 0))).astype(f32)
    dhor = middle.astype(bf16).reshape(x_local, v_all, s_h, 2, channels)
    dhor = jnp.transpose(dhor, (3, 2, 0, 1, 4)).reshape(features.shape)

    packed = jnp.concatenate([packed_h, packed_v], axis=0)
    summed = sum_over_devices(packed, rows, cols).reshape(2, 5, channels, 2, channels)
    factor = float(u_all * v_all * y_all * x_all) ** (-0.5)
    summed = summed * factor
    raw_beta = summed[:, 4, :count, 1]
    by_tap = jnp.transpose(summed, (0, 4, 2, 1, 3)).reshape(2, channels, channels, 10)
    by_tap = by_tap[..., :9].reshape(2, channels, channels, 3, 3)
    grad_beta = jnp.sum(chosen[None, :, :, None] * raw_beta[:, :, None], axis=1)
    return output, dhor, by_tap[0], by_tap[1], grad_beta[0], grad_beta[1]


def solution(mesh):
    placed = (P("vrow", None, "img", None), P(), P(), P(), P(), P(), P("vrow", "img", None))
    return jax.shard_map(
        per_device,
        mesh=mesh,
        in_specs=placed,
        out_specs=(P("vrow", "img", None), P("vrow", None, "img", None), P(), P(), P(), P()),
        check_vma=False,
    )
```

```python
import functools

import jax
import jax.numpy as jnp
from jax import lax
from jax.experimental import pallas as pl
from jax.experimental.pallas import tpu as pltpu
from jax.sharding import PartitionSpec as P

SHIFTS = (-2, -1, 0, 1, 2)
REACH = 3
TAPS = tuple((i, j) for i in (-1, 0, 1) for j in (-1, 0, 1))
LANES = 128
MESH = pl.DeviceIdType.MESH
VMEM_LIMIT = 60 * 1024 * 1024


def place_of(x, shift, shape, start):
    views = lax.broadcasted_iota(jnp.int32, shape, 0) - shape[0] // 2
    return start + x - shift * views


def tap_products(f_ref, w_ref, which, z_ref, first, length):
    _, _, nv2, s, _ = z_ref.shape
    nv = nv2 - 2
    source = f_ref[first : first + length].reshape(length * nv * s, LANES)
    for t in range(0, 9, 2):
        last = min(t + 2, 9)
        got = jnp.dot(
            source, w_ref[which, :, t * LANES : last * LANES], preferred_element_type=jnp.float32
        )
        for k in range(t, last):
            part = got[:, (k - t) * LANES : (k - t + 1) * LANES]
            z_ref[k, first : first + length, 1 : nv + 1] = part.reshape(length, nv, s, LANES)


def clear_products(z_ref):
    _, nxe, nv2, s, _ = z_ref.shape
    zero = jnp.zeros((9, nxe, 1, s, LANES), jnp.float32)
    z_ref[:, :, 0:1] = zero
    z_ref[:, :, nv2 - 1 : nv2] = zero


def preact_at(z_ref, x, index, shift, place, total):
    nv = z_ref.shape[2] - 2
    sums = {}
    for t, (i, j) in enumerate(TAPS):
        term = z_ref[t, x + (REACH + j + shift * i), 1 + i : 1 + i + nv]
        sums[j] = term if j not in sums else sums[j] + term
    low = jnp.where(place != 0, sums[-1], 0.0)
    high = jnp.where(place != total - 1, sums[1], 0.0)
    return sums[0] + low + high


def sigma_of(p):
    return 0.5 * jnp.tanh(0.5 * p) + 0.5


def store_dpre(d_ref, r_ref, x, index, place, total, keep, grad, blend, p, sigma):
    nv = grad.shape[0]
    act = jnp.where(keep, p * sigma, 0.0)
    r_ref[index] += jnp.sum(grad * act, axis=0)
    slope = sigma * (1.0 + p * (1.0 - sigma))
    dpre = jnp.where(keep, blend * grad * slope, 0.0)
    d_ref[0, index, x, 1 : nv + 1] = jnp.where(place != 0, dpre, 0.0)
    d_ref[1, index, x, 1 : nv + 1] = dpre
    d_ref[2, index, x, 1 : nv + 1] = jnp.where(place != total - 1, dpre, 0.0)


def clear_dpre(d_ref, r_ref, nx, pad):
    _, count, _, nv2, s, _ = d_ref.shape
    r_ref[...] = jnp.zeros_like(r_ref)
    for j in range(3):
        rim = jnp.zeros((count, pad, nv2, s, LANES), jnp.float32)
        d_ref[j, :, 0:pad] = rim
        d_ref[j, :, pad + nx : 2 * pad + nx] = rim
        side = jnp.zeros((count, nx, 1, s, LANES), jnp.float32)
        d_ref[j, :, pad : pad + nx, 0:1] = side
        d_ref[j, :, pad : pad + nx, nv2 - 1 : nv2] = side


def gather_dpre(d_ref, s_ref, length):
    nv2, s = d_ref.shape[3:5]
    nv = nv2 - 2

    def body(x, carry):
        for t, (i, j) in enumerate(TAPS):
            total = None
            for index, shift in enumerate(SHIFTS):
                term = d_ref[j + 1, index, x + (REACH - j - shift * i), 1 - i : 1 - i + nv]
                total = term if total is None else total + term
            here = pl.ds(pl.multiple_of(x * (nv * s), 16), nv * s)
            s_ref[here, t * LANES : (t + 1) * LANES] = total.reshape(nv * s, LANES).astype(
                jnp.bfloat16
            )
        return carry

    lax.fori_loop(0, length, body, 0)


def pack_grads(source, stacked, r_ref, out_ref, which):
    wide = lax.dot_general(
        source, stacked, (((0,), (0,)), ((), ())), preferred_element_type=jnp.float32
    )
    half = LANES // 2
    first, second = wide[:half], wide[half:]
    left = lax.broadcasted_iota(jnp.int32, (half, LANES), 1) < half
    sums = jnp.sum(r_ref[...], axis=1)
    sums = sums + pltpu.roll(sums, half, 1)
    for m in range(5):
        low = slice(2 * m * LANES, (2 * m + 1) * LANES)
        even = first[:, low] + pltpu.roll(second[:, low], half, 1)
        if m < 4:
            high = slice((2 * m + 1) * LANES, (2 * m + 2) * LANES)
            odd = pltpu.roll(first[:, high], half, 1) + second[:, high]
        else:
            odd = jnp.concatenate(
                [sums, jnp.zeros((half - sums.shape[0], LANES), jnp.float32)], axis=0
            )
        out_ref[which, m * half : (m + 1) * half] = jnp.where(left, even, odd)


def half_roll(x):
    return pltpu.roll(x, LANES // 2, x.ndim - 1)


def remote(src, dst, sems, k, device):
    return pltpu.make_async_remote_copy(
        src_ref=src,
        dst_ref=dst,
        send_sem=sems.at[0, k],
        recv_sem=sems.at[1, k],
        device_id=device,
        device_id_type=MESH,
    )


class Sum:
    def __init__(self, rows, cols, x_ref, o_ref, heard, totals, sem_a, sem_b, sem_c):
        self.rows, self.cols = rows, cols
        self.x_ref, self.o_ref, self.heard, self.totals = x_ref, o_ref, heard, totals
        self.sems = (sem_a, sem_b, sem_c)
        self.row, self.col = lax.axis_index("vrow"), lax.axis_index("img")
        self.size = heard.shape[1]
        self.sent = []

    def chunk(self, index):
        return pl.ds(pl.multiple_of(index * self.size, 8), self.size)

    def scatter(self):
        self.first = []
        for k in range(1, self.cols):
            to = lax.rem(self.col + k, self.cols)
            source = self.x_ref.at[self.chunk(to)]
            copy = remote(source, self.heard.at[k - 1], self.sems[0], k - 1, (self.row, to))
            copy.start()
            self.first.append(copy)

    def exchange(self):
        total = self.x_ref[self.chunk(self.col)]
        for k, copy in enumerate(self.first):
            copy.wait_recv()
            total = total + self.heard[k]
        self.totals[self.row] = total
        self.second = []
        for k in range(1, self.rows):
            to = lax.rem(self.row + k, self.rows)
            mine = self.totals.at[self.row]
            copy = remote(mine, mine, self.sems[1], k - 1, (to, self.col))
            copy.start()
            self.second.append(copy)

    def gather(self):
        for copy in self.second:
            copy.wait_recv()
        total = self.totals[0]
        for k in range(1, self.rows):
            total = total + self.totals[k]
        self.o_ref[self.chunk(self.col)] = total
        self.third = []
        for k in range(1, self.cols):
            to = lax.rem(self.col + k, self.cols)
            mine = self.o_ref.at[self.chunk(self.col)]
            copy = remote(mine, mine, self.sems[2], k - 1, (self.row, to))
            copy.start()
            self.third.append(copy)

    def finish(self):
        for copy in self.third:
            copy.wait_recv()
        for copy in self.first + self.second + self.third:
            copy.wait_send()


def field_kernel(
    rows,
    cols,
    f_ref,
    c_ref,
    w_ref,
    b_ref,
    o_ref,
    dhor_ref,
    sum_ref,
    wide,
    pre_ref,
    hfeat,
    send_h,
    got_h,
    vert,
    dvert,
    send_v,
    got_v,
    grad_h,
    rim_sent,
    rim_got,
    payload,
    heard,
    totals,
    s_ref,
    r_h,
    r_v,
    halo_sem,
    there_sem,
    back_sem,
    rim_sem,
    sum_a,
    sum_b,
    sum_c,
):
    row, col = lax.axis_index("vrow"), lax.axis_index("img")
    _, nx, nv, s, _ = pre_ref.shape
    ny, nu, sv, _ = dvert.shape
    x_all = nx * cols
    start = col * nx
    count = len(SHIFTS)
    f32, bf16 = jnp.float32, jnp.bfloat16
    left = lax.broadcasted_iota(jnp.int32, (1, 1, LANES), 2) < LANES // 2
    right_col, left_col = lax.rem(col + 1, cols), lax.rem(col + cols - 1, cols)

    barrier = pltpu.get_barrier_semaphore()
    for k in range(1, cols):
        peer = (row, lax.rem(col + k, cols))
        pl.semaphore_signal(barrier, inc=1, device_id=peer, device_id_type=MESH)
    for k in range(1, rows):
        peer = (lax.rem(row + k, rows), col)
        pl.semaphore_signal(barrier, inc=1, device_id=peer, device_id_type=MESH)
    pl.semaphore_wait(barrier, cols + rows - 2)

    halo = [
        remote(
            f_ref.at[pl.ds(nx - REACH, REACH)],
            wide.at[pl.ds(0, REACH)],
            halo_sem,
            0,
            (row, right_col),
        ),
        remote(
            f_ref.at[pl.ds(0, REACH)],
            wide.at[pl.ds(nx + REACH, REACH)],
            halo_sem,
            1,
            (row, left_col),
        ),
    ]
    for copy in halo:
        copy.start()

    for copy in halo:
        copy.wait_recv()

    @pl.when(col == 0)
    def _():
        wide[:REACH] = jnp.zeros((REACH,) + wide.shape[1:], bf16)

    @pl.when(col == cols - 1)
    def _():
        wide[nx + REACH :] = jnp.zeros((REACH,) + wide.shape[1:], bf16)

    wide[REACH : REACH + nx] = f_ref[...]
    there = []

    def first_pass(z_ref):
        clear_products(z_ref)
        tap_products(wide, w_ref, 0, z_ref, 0, nx + 2 * REACH)

        def body(x, carry):
            out = f_ref[x].astype(f32).reshape(nv, s, LANES)
            for index, shift in enumerate(SHIFTS):
                place = place_of(x, shift, (nv, s, LANES), start)
                p = preact_at(z_ref, x, index, shift, place, x_all)
                pre_ref[index, x] = p
                keep = (place >= 0) & (place < x_all)
                out = out + b_ref[0, index : index + 1] * jnp.where(keep, p * sigma_of(p), 0.0)
            hfeat[x] = out
            return carry

        lax.fori_loop(0, nx, body, 0)

    pl.run_scoped(first_pass, pltpu.VMEM((9, nx + 2 * REACH, nv + 2, s, LANES), f32))

    def block_there(to):
        views = hfeat[:, pl.ds(2 * to, 2)]
        one, two = views[:, 0], views[:, 1]
        low = jnp.swapaxes(jnp.where(left, one, half_roll(two)), 0, 1)
        high = jnp.swapaxes(jnp.where(left, half_roll(one), two), 0, 1)
        return jnp.concatenate([low, high], axis=0).reshape(ny * sv, LANES).astype(bf16)

    for k in range(1, rows):
        to = lax.rem(row + k, rows)
        send_h[k - 1] = block_there(to)
        copy = remote(send_h.at[k - 1], got_h.at[row], there_sem, k - 1, (to, col))
        copy.start()
        there.append(copy)
    got_h[row] = block_there(row)

    sum_v = Sum(
        rows,
        cols,
        payload.at[1],
        sum_ref.at[1],
        heard.at[1],
        totals.at[1],
        sum_a.at[1],
        sum_b.at[1],
        sum_c.at[1],
    )
    sum_h = Sum(
        rows,
        cols,
        payload.at[0],
        sum_ref.at[0],
        heard.at[0],
        totals.at[0],
        sum_a.at[0],
        sum_b.at[0],
        sum_c.at[0],
    )
    back = []

    for copy in there:
        copy.wait_recv()
    parts = [got_h[u].astype(f32).reshape(ny, 1, sv, LANES) for u in range(rows)]
    vert[REACH : REACH + ny] = (
        jnp.concatenate(parts, axis=1).reshape(ny, nu * sv, LANES).astype(bf16)
    )

    def second_pass(z_ref, d_ref):
        clear_products(z_ref)
        clear_dpre(d_ref, r_v, ny, REACH)
        vert[:REACH] = jnp.zeros((REACH,) + vert.shape[1:], bf16)
        vert[ny + REACH :] = jnp.zeros((REACH,) + vert.shape[1:], bf16)
        rim = jnp.zeros((9, REACH, nu, sv, LANES), f32)
        z_ref[:, :REACH, 1 : nu + 1] = rim
        z_ref[:, ny + REACH :, 1 : nu + 1] = rim
        tap_products(vert, w_ref, 1, z_ref, REACH, ny)

        def body(y, carry):
            out = vert[y + REACH].astype(f32).reshape(nu, sv, LANES)
            grad = c_ref[y].astype(f32).reshape(nu, sv, LANES)
            for index, shift in enumerate(SHIFTS):
                place = place_of(y, shift, (nu, sv, LANES), 0)
                p = preact_at(z_ref, y, index, shift, place, ny)
                sigma = sigma_of(p)
                keep = (place >= 0) & (place < ny)
                blend = b_ref[1, index : index + 1]
                out = out + blend * jnp.where(keep, p * sigma, 0.0)
                store_dpre(
                    d_ref, r_v, y + REACH, index, place, ny, keep, grad, blend, p, sigma
                )
            o_ref[y] = out.reshape(nu * sv, LANES).astype(bf16)
            return carry

        lax.fori_loop(0, ny, body, 0)
        gather_dpre(d_ref, s_ref, ny)

    pl.run_scoped(
        second_pass,
        pltpu.VMEM((9, ny + 2 * REACH, nu + 2, sv, LANES), f32),
        pltpu.VMEM((3, count, ny + 2 * REACH, nu + 2, sv, LANES), f32),
    )
    stacked = s_ref[: ny * nu * sv]
    grads = lax.dot_general(
        stacked, w_ref[1], (((1,), (1,)), ((), ())), preferred_element_type=f32
    )
    dvert[...] = c_ref[...].astype(f32).reshape(dvert.shape) + grads.reshape(dvert.shape)

    def block_back(to):
        block = dvert[:, pl.ds(to, 1)].reshape(ny, sv, LANES)
        low = jnp.swapaxes(block[:s], 0, 1)
        high = jnp.swapaxes(block[s:], 0, 1)
        one = jnp.where(left, low, half_roll(high))
        two = jnp.where(left, half_roll(low), high)
        both = jnp.concatenate([one[:, None], two[:, None]], axis=1)
        return both.reshape(nx, 2 * s, LANES).astype(bf16)

    for k in range(1, rows):
        to = lax.rem(row + k, rows)
        send_v[k - 1] = block_back(to)
        copy = remote(send_v.at[k - 1], got_v.at[row], back_sem, k - 1, (to, col))
        copy.start()
        back.append(copy)
    got_v[row] = block_back(row)
    source = vert[REACH : REACH + ny].reshape(ny * nu * sv, LANES)
    pack_grads(source, stacked, r_v, payload, 1)
    sum_v.scatter()


    for copy in back:
        copy.wait_recv()
    for r in range(rows):
        grad_h[:, r * 2 * s : (r + 1) * 2 * s] = got_v[r].astype(f32)

    def third_pass(d_ref):
        clear_dpre(d_ref, r_h, nx, 2 * REACH)
        def body(x, carry):
            grad = grad_h[x].reshape(nv, s, LANES)
            for index, shift in enumerate(SHIFTS):
                place = place_of(x, shift, (nv, s, LANES), start)
                p = pre_ref[index, x]
                keep = (place >= 0) & (place < x_all)
                blend = b_ref[0, index : index + 1]
                sigma = sigma_of(p)
                store_dpre(
                    d_ref,
                    r_h,
                    x + 2 * REACH,
                    index,
                    place,
                    x_all,
                    keep,
                    grad,
                    blend,
                    p,
                    sigma,
                )
            return carry

        lax.fori_loop(0, nx, body, 0)
        gather_dpre(d_ref, s_ref, nx + 2 * REACH)

    pl.run_scoped(
        third_pass,
        pltpu.VMEM((3, count, nx + 4 * REACH, nv + 2, s, LANES), f32),
    )
    sum_v.exchange()
    stacked = s_ref[: (nx + 2 * REACH) * nv * s]
    source = wide[...].reshape((nx + 2 * REACH) * nv * s, LANES)
    pack_grads(source, stacked, r_h, payload, 0)
    sum_h.scatter()
    sum_v.gather()
    grads = lax.dot_general(
        stacked, w_ref[0], (((1,), (1,)), ((), ())), preferred_element_type=f32
    ).reshape(nx + 2 * REACH, nv * s, LANES)
    rim_sent[0] = grads[:REACH].astype(bf16)
    rim_sent[1] = grads[nx + REACH :].astype(bf16)
    grad_h[...] += grads[REACH : REACH + nx]

    rims = [
        remote(rim_sent.at[0], rim_got.at[1], rim_sem, 0, (row, left_col)),
        remote(rim_sent.at[1], rim_got.at[0], rim_sem, 1, (row, right_col)),
    ]
    for copy in rims:
        copy.start()
    sum_h.exchange()
    for copy in rims:
        copy.wait_recv()

    @pl.when(col > 0)
    def _():
        grad_h[:REACH] += rim_got[0].astype(f32)

    @pl.when(col < cols - 1)
    def _():
        grad_h[nx - REACH :] += rim_got[1].astype(f32)

    dhor_ref[...] = grad_h[...].astype(bf16)
    sum_h.gather()
    for copy in halo + there + back + rims:
        copy.wait_send()
    sum_v.finish()
    sum_h.finish()


def per_device(features, weight_h, weight_v, beta_h, beta_v, shear_set, cotangent):
    rows, cols = lax.axis_size("vrow"), lax.axis_size("img")
    channels = weight_h.shape[0]
    u_local, y_all, x_local, merged = features.shape
    v_all = merged // channels
    v_local = v_all // rows
    u_all = u_local * rows
    x_all = x_local * cols
    s_h = u_local * y_all // 2
    s_v = v_local * x_local // 2
    f32, bf16 = jnp.float32, jnp.bfloat16
    count = len(SHIFTS)
    assert u_local == 1 and v_local == 2

    weights = jnp.stack([weight_h, weight_v]).reshape(2, channels, channels, 9)
    weights = jnp.transpose(weights, (0, 2, 3, 1))
    eye = jnp.eye(2, dtype=bf16)
    weights = weights[:, None, :, :, None, :] * eye[None, :, None, None, :, None]
    weights = weights.reshape(2, LANES, 9 * LANES)
    chosen = (jnp.asarray(SHIFTS, jnp.int32)[:, None] == shear_set[None, :]).astype(f32)
    betas = jnp.stack([beta_h, beta_v])
    blends = jnp.sum(chosen[None, :, :, None] * betas[:, None], axis=2)
    blends = jnp.tile(blends, (1, 1, 2))

    field = features.reshape(2, s_h, x_local, v_all, channels)
    field = jnp.transpose(field, (2, 3, 1, 0, 4)).reshape(x_local, v_all * s_h, LANES)
    grad_v = cotangent.reshape(2, s_v, u_all, y_all, channels)
    grad_v = jnp.transpose(grad_v, (3, 2, 1, 0, 4)).reshape(y_all, u_all * s_v, LANES)
    flat_h = (x_local, v_all * s_h, LANES)
    flat_v = (y_all, u_all * s_v, LANES)
    rim = (REACH, v_all * s_h, LANES)
    grads = 5 * channels
    chunk = (grads // cols, LANES)
    vmem, dma = pltpu.VMEM, pltpu.SemaphoreType.DMA
    whole = pl.BlockSpec(memory_space=vmem)
    vout, dhor, summed = pl.pallas_call(
        functools.partial(field_kernel, rows, cols),
        out_shape=[
            jax.ShapeDtypeStruct(flat_v, bf16),
            jax.ShapeDtypeStruct(flat_h, bf16),
            jax.ShapeDtypeStruct((2, grads, LANES), f32),
        ],
        in_specs=[whole] * 4,
        out_specs=[whole] * 3,
        scratch_shapes=[
            vmem((x_local + 2 * REACH,) + flat_h[1:], bf16),
            vmem((count, x_local, v_all, s_h, LANES), f32),
            vmem((x_local, v_all, s_h, LANES), f32),
            vmem((rows - 1, y_all * s_v, LANES), bf16),
            vmem((rows, y_all * s_v, LANES), bf16),
            vmem((y_all + 2 * REACH,) + flat_v[1:], bf16),
            vmem((y_all, u_all, s_v, LANES), f32),
            vmem((rows - 1, x_local, 2 * s_h, LANES), bf16),
            vmem((rows, x_local, 2 * s_h, LANES), bf16),
            vmem(flat_h, f32),
            vmem((2,) + rim, bf16),
            vmem((2,) + rim, bf16),
            vmem((2, grads, LANES), f32),
            vmem((2, cols - 1) + chunk, f32),
            vmem((2, rows) + chunk, f32),
            vmem((max((x_local + 2 * REACH) * flat_h[1], y_all * flat_v[1]), 9 * LANES), bf16),
            vmem((count, s_h, LANES), f32),
            vmem((count, s_v, LANES), f32),
            dma((2, 2)),
            dma((2, rows - 1)),
            dma((2, rows - 1)),
            dma((2, 2)),
            dma((2, 2, cols - 1)),
            dma((2, 2, rows - 1)),
            dma((2, 2, cols - 1)),
        ],
        compiler_params=pltpu.CompilerParams(
            collective_id=0, has_side_effects=True, vmem_limit_bytes=VMEM_LIMIT
        ),
        name="light_field",
    )(field, grad_v, weights, blends)
    output = jnp.transpose(vout.reshape(y_all, u_all, s_v, 2, channels), (3, 2, 1, 0, 4))
    output = output.reshape(v_local, x_local, u_all * y_all * channels)
    dhor = dhor.reshape(x_local, v_all, s_h, 2, channels)
    dhor = jnp.transpose(dhor, (3, 2, 0, 1, 4)).reshape(features.shape)
    summed = summed.reshape(2, 5, channels, 2, channels)
    factor = float(u_all * v_all * y_all * x_all) ** (-0.5)
    summed = summed * factor
    raw_beta = summed[:, 4, :count, 1]
    by_tap = jnp.transpose(summed, (0, 4, 2, 1, 3)).reshape(2, channels, channels, 10)
    by_tap = by_tap[..., :9].reshape(2, channels, channels, 3, 3)
    grad_beta = jnp.sum(chosen[None, :, :, None] * raw_beta[:, :, None], axis=1)
    return output, dhor, by_tap[0], by_tap[1], grad_beta[0], grad_beta[1]


def solution(mesh):
    placed = (P("vrow", None, "img", None), P(), P(), P(), P(), P(), P("vrow", "img", None))
    return jax.shard_map(
        per_device,
        mesh=mesh,
        in_specs=placed,
        out_specs=(P("vrow", "img", None), P("vrow", None, "img", None), P(), P(), P(), P()),
        check_vma=False,
    )
```

```python
import functools

import jax
import jax.numpy as jnp
from jax import lax
from jax.experimental import pallas as pl
from jax.experimental.pallas import tpu as pltpu
from jax.sharding import PartitionSpec as P

SHIFTS = (-2, -1, 0, 1, 2)
REACH = 3
TAPS = tuple((i, j) for i in (-1, 0, 1) for j in (-1, 0, 1))
LANES = 128
MESH = pl.DeviceIdType.MESH
VMEM_LIMIT = 60 * 1024 * 1024


def place_of(x, shift, views, shape, start):
    view = lax.broadcasted_iota(jnp.int32, shape, 0) // (shape[0] // views) - views // 2
    return start + x - shift * view


def dot_t(x, y):
    return lax.dot_general(x, y, (((1,), (1,)), ((), ())), preferred_element_type=jnp.float32)


def tap_products(f_ref, w_ref, which, z_ref, views, first, length):
    rows = f_ref.shape[1]
    per = rows // 8
    step = per // views * (views + 2)
    source = f_ref[first : first + length].reshape(length * rows, LANES)
    for t in range(0, 9, 2):
        last = min(t + 2, 9)
        got = dot_t(source, w_ref[which, t * LANES : last * LANES])
        for k in range(t, last):
            part = got[:, (k - t) * LANES : (k - t + 1) * LANES]
            for x in range(length):
                here = (first + x) * step + per // views
                z_ref[k, here : here + per] = part[x * rows : (x + 1) * rows].reshape(
                    per, 8, LANES
                )


def clear_products(z_ref, columns, views, group, rim):
    step = (views + 2) * group
    side = jnp.zeros((9, group, 8, LANES), jnp.float32)

    def body(x, carry):
        z_ref[:, pl.ds(x * step, group)] = side
        z_ref[:, pl.ds(x * step + (views + 1) * group, group)] = side
        return carry

    lax.fori_loop(0, columns, body, 0)
    if rim:
        zero = jnp.zeros((9, rim * step, 8, LANES), jnp.float32)
        z_ref[:, : rim * step] = zero
        z_ref[:, (columns - rim) * step : columns * step] = zero


def preact_at(z_ref, x, views, group, shift, place, total):
    step = (views + 2) * group
    sums = {}
    for t, (i, j) in enumerate(TAPS):
        here = (x + (REACH + j + shift * i)) * step + (1 + i) * group
        term = z_ref[t, pl.ds(here, views * group)]
        sums[j] = term if j not in sums else sums[j] + term
    low = jnp.where(place != 0, sums[-1], 0.0)
    high = jnp.where(place != total - 1, sums[1], 0.0)
    return sums[0] + low + high


def sigma_of(p):
    return 0.5 * jnp.tanh(0.5 * p) + 0.5


def store_dpre(d_ref, r_ref, x, index, group, keep, grad, blend, p, sigma):
    act = jnp.where(keep, p * sigma, 0.0)
    r_ref[index] += jnp.sum(grad * act, axis=0)
    slope = sigma * (1.0 + p * (1.0 - sigma))
    dpre = jnp.where(keep, blend * grad * slope, 0.0)
    d_ref[index, x, group : group + grad.shape[0]] = dpre


def clear_dpre(d_ref, r_ref, nx, pad, group):
    count, _, per, _, _ = d_ref.shape
    r_ref[...] = jnp.zeros_like(r_ref)
    rim = jnp.zeros((count, pad, per, 8, LANES), jnp.float32)
    d_ref[:, 0:pad] = rim
    d_ref[:, pad + nx : 2 * pad + nx] = rim
    side = jnp.zeros((count, nx, group, 8, LANES), jnp.float32)
    d_ref[:, pad : pad + nx, 0:group] = side
    d_ref[:, pad : pad + nx, per - group : per] = side


def gather_dpre(d_ref, s_ref, length, views, group, start, total):
    per = views * group

    def body(x, carry):
        sums = [None] * 9
        for index, shift in enumerate(SHIFTS):
            place = place_of(x, shift, views, (per, 8, LANES), start)
            inside = (place >= 0) & (place < total)
            for t, (i, j) in enumerate(TAPS):
                term = d_ref[
                    index, x + (REACH - j - shift * i), (1 - i) * group : (1 - i) * group + per
                ]
                if j != 0:
                    term = jnp.where(inside, term, 0.0)
                sums[t] = term if sums[t] is None else sums[t] + term
        here = pl.ds(pl.multiple_of(x * (per * 8), 16), per * 8)
        for t in range(9):
            s_ref[here, t * LANES : (t + 1) * LANES] = (
                sums[t].reshape(per * 8, LANES).astype(jnp.bfloat16)
            )
        return carry

    lax.fori_loop(0, length, body, 0)


def pack_grads(source, stacked, r_ref, out_ref, which):
    wide = lax.dot_general(
        source, stacked, (((0,), (0,)), ((), ())), preferred_element_type=jnp.float32
    )
    half = LANES // 2
    first, second = wide[:half], wide[half:]
    left = lax.broadcasted_iota(jnp.int32, (half, LANES), 1) < half
    sums = jnp.sum(r_ref[...], axis=1)
    sums = sums + pltpu.roll(sums, half, 1)
    for m in range(5):
        low = slice(2 * m * LANES, (2 * m + 1) * LANES)
        even = first[:, low] + pltpu.roll(second[:, low], half, 1)
        if m < 4:
            high = slice((2 * m + 1) * LANES, (2 * m + 2) * LANES)
            odd = pltpu.roll(first[:, high], half, 1) + second[:, high]
        else:
            odd = jnp.concatenate(
                [sums, jnp.zeros((half - sums.shape[0], LANES), jnp.float32)], axis=0
            )
        out_ref[which, m * half : (m + 1) * half] = jnp.where(left, even, odd)


def exchange_halves(one, two, left):
    return jnp.where(left, one, half_roll(two)), jnp.where(left, half_roll(one), two)


def stack_weights(weight_ref, w_ref, which, left):
    half = LANES // 2
    for t in range(9):
        tap = weight_ref[t].astype(jnp.float32)
        twice = jnp.concatenate([tap, tap], axis=1)
        both = jnp.concatenate(
            [jnp.where(left, twice, 0.0), jnp.where(left, 0.0, twice)], axis=0
        )
        w_ref[which, t * LANES : (t + 1) * LANES] = both.astype(jnp.bfloat16)


def stack_blends(beta_ref, shear_ref, b_ref, which):
    beta = beta_ref[...]
    beta = jnp.concatenate([beta, beta], axis=1)
    for index, shift in enumerate(SHIFTS):
        total = jnp.zeros((1, LANES), jnp.float32)
        for k in range(beta.shape[0]):
            total = total + jnp.where(shear_ref[k] == shift, 1.0, 0.0) * beta[k : k + 1]
        b_ref[which, index : index + 1] = total


def unpack_grads(sum_ref, which, shear_ref, weight_ref, beta_ref, factor):
    half = LANES // 2
    for m in range(5):
        tile = sum_ref[which, m * half : (m + 1) * half] * factor
        turned = jnp.transpose(tile)
        weight_ref[2 * m] = turned[:half]
        if m < 4:
            weight_ref[2 * m + 1] = turned[half:]
        else:
            raw = half_roll(tile[:8])[:, :half]
    for k in range(beta_ref.shape[0]):
        total = jnp.zeros((1, half), jnp.float32)
        for index, shift in enumerate(SHIFTS):
            total = total + jnp.where(shear_ref[k] == shift, 1.0, 0.0) * raw[index : index + 1]
        beta_ref[k : k + 1] = total


def half_roll(x):
    return pltpu.roll(x, LANES // 2, x.ndim - 1)


def remote(src, dst, sems, k, device):
    return pltpu.make_async_remote_copy(
        src_ref=src,
        dst_ref=dst,
        send_sem=sems.at[0, k],
        recv_sem=sems.at[1, k],
        device_id=device,
        device_id_type=MESH,
    )


class Sum:
    def __init__(self, rows, cols, x_ref, o_ref, heard, totals, sem_a, sem_b, sem_c):
        self.rows, self.cols = rows, cols
        self.x_ref, self.o_ref, self.heard, self.totals = x_ref, o_ref, heard, totals
        self.sems = (sem_a, sem_b, sem_c)
        self.row, self.col = lax.axis_index("vrow"), lax.axis_index("img")
        self.size = heard.shape[1]
        self.sent = []

    def chunk(self, index):
        return pl.ds(pl.multiple_of(index * self.size, 8), self.size)

    def scatter(self):
        self.first = []
        for k in range(1, self.cols):
            to = lax.rem(self.col + k, self.cols)
            source = self.x_ref.at[self.chunk(to)]
            copy = remote(source, self.heard.at[k - 1], self.sems[0], k - 1, (self.row, to))
            copy.start()
            self.first.append(copy)

    def exchange(self):
        total = self.x_ref[self.chunk(self.col)]
        for k, copy in enumerate(self.first):
            copy.wait_recv()
            total = total + self.heard[k]
        self.totals[self.row] = total
        self.second = []
        for k in range(1, self.rows):
            to = lax.rem(self.row + k, self.rows)
            mine = self.totals.at[self.row]
            copy = remote(mine, mine, self.sems[1], k - 1, (to, self.col))
            copy.start()
            self.second.append(copy)

    def gather(self):
        for copy in self.second:
            copy.wait_recv()
        total = self.totals[0]
        for k in range(1, self.rows):
            total = total + self.totals[k]
        self.o_ref[self.chunk(self.col)] = total
        self.third = []
        for k in range(1, self.cols):
            to = lax.rem(self.col + k, self.cols)
            mine = self.o_ref.at[self.chunk(self.col)]
            copy = remote(mine, mine, self.sems[2], k - 1, (self.row, to))
            copy.start()
            self.third.append(copy)

    def finish(self):
        for copy in self.third:
            copy.wait_recv()
        for copy in self.first + self.second + self.third:
            copy.wait_send()


def field_kernel(
    rows,
    cols,
    f_ref,
    weight_h_ref,
    weight_v_ref,
    beta_h_ref,
    beta_v_ref,
    shear_ref,
    c_ref,
    o_ref,
    dhor_ref,
    gw_h_ref,
    gw_v_ref,
    gb_h_ref,
    gb_v_ref,
    wide,
    w_ref,
    b_ref,
    z_ref,
    pre_ref,
    hfeat,
    send_h,
    got_h,
    vert,
    cot,
    vout,
    dvert,
    send_v,
    got_v,
    grad_h,
    rim_sent,
    rim_got,
    payload,
    sum_ref,
    heard,
    totals,
    s_ref,
    d_h,
    d_v,
    r_h,
    r_v,
    halo_sem,
    there_sem,
    back_sem,
    rim_sem,
    sum_a,
    sum_b,
    sum_c,
):
    row, col = lax.axis_index("vrow"), lax.axis_index("img")
    nx, nvs, _ = grad_h.shape
    ny, nu, sv, _ = dvert.shape
    s = f_ref.shape[0] // 2
    nv = nvs // s
    gh, gv = s // 8, sv // 8
    x_all = nx * cols
    start = col * nx
    f32, bf16 = jnp.float32, jnp.bfloat16
    shape_h, shape_v = (nv * gh, 8, LANES), (nu * gv, 8, LANES)
    left = lax.broadcasted_iota(jnp.int32, (1, 1, LANES), 2) < LANES // 2
    left2 = lax.broadcasted_iota(jnp.int32, (1, LANES), 1) < LANES // 2
    right_col, left_col = lax.rem(col + 1, cols), lax.rem(col + cols - 1, cols)

    barrier = pltpu.get_barrier_semaphore()
    for k in range(1, cols):
        peer = (row, lax.rem(col + k, cols))
        pl.semaphore_signal(barrier, inc=1, device_id=peer, device_id_type=MESH)
    for k in range(1, rows):
        peer = (lax.rem(row + k, rows), col)
        pl.semaphore_signal(barrier, inc=1, device_id=peer, device_id_type=MESH)

    for m in range(nv // 2):
        block = f_ref[:, :, m * LANES : (m + 1) * LANES].astype(f32)
        low, high = jnp.swapaxes(block[:s], 0, 1), jnp.swapaxes(block[s:], 0, 1)
        both = jnp.concatenate(exchange_halves(low, high, left), axis=1)
        wide[REACH : REACH + nx, m * 2 * s : (m + 1) * 2 * s] = both.astype(bf16)
    pl.semaphore_wait(barrier, cols + rows - 2)

    halo = [
        remote(
            wide.at[pl.ds(nx, REACH)],
            wide.at[pl.ds(0, REACH)],
            halo_sem,
            0,
            (row, right_col),
        ),
        remote(
            wide.at[pl.ds(REACH, REACH)],
            wide.at[pl.ds(nx + REACH, REACH)],
            halo_sem,
            1,
            (row, left_col),
        ),
    ]
    for copy in halo:
        copy.start()
    stack_weights(weight_h_ref, w_ref, 0, left2)
    stack_blends(beta_h_ref, shear_ref, b_ref, 0)
    clear_products(z_ref, nx + 2 * REACH, nv, gh, 0)
    tap_products(wide, w_ref, 0, z_ref, nv, REACH, nx)
    for copy in halo:
        copy.wait_recv()

    @pl.when(col == 0)
    def _():
        wide[:REACH] = jnp.zeros((REACH, nvs, LANES), bf16)

    @pl.when(col == cols - 1)
    def _():
        wide[nx + REACH :] = jnp.zeros((REACH, nvs, LANES), bf16)

    tap_products(wide, w_ref, 0, z_ref, nv, 0, REACH)
    tap_products(wide, w_ref, 0, z_ref, nv, nx + REACH, REACH)

    def first_pass(x, carry):
        out = wide[x + REACH].astype(f32).reshape(shape_h)
        for index, shift in enumerate(SHIFTS):
            place = place_of(x, shift, nv, shape_h, start)
            p = preact_at(z_ref, x, nv, gh, shift, place, x_all)
            pre_ref[index, x] = p
            keep = (place >= 0) & (place < x_all)
            out = out + b_ref[0, index : index + 1] * jnp.where(keep, p * sigma_of(p), 0.0)
        hfeat[x] = out.reshape(nv, s, LANES)
        return carry

    lax.fori_loop(0, nx, first_pass, 0)

    def block_there(to):
        views = hfeat[:, pl.ds(2 * to, 2)]
        low, high = exchange_halves(views[:, 0], views[:, 1], left)
        both = [jnp.swapaxes(low, 0, 1), jnp.swapaxes(high, 0, 1)]
        return jnp.concatenate(both, axis=0).reshape(ny * sv, LANES).astype(bf16)

    there = []
    for k in range(1, rows):
        to = lax.rem(row + k, rows)
        send_h[k - 1] = block_there(to)
        copy = remote(send_h.at[k - 1], got_h.at[row], there_sem, k - 1, (to, col))
        copy.start()
        there.append(copy)
    got_h[row] = block_there(row)

    sum_h, sum_v = [
        Sum(
            rows,
            cols,
            payload.at[n],
            sum_ref.at[n],
            heard.at[n],
            totals.at[n],
            sum_a.at[n],
            sum_b.at[n],
            sum_c.at[n],
        )
        for n in range(2)
    ]
    stack_weights(weight_v_ref, w_ref, 1, left2)
    stack_blends(beta_v_ref, shear_ref, b_ref, 1)
    clear_products(z_ref, ny + 2 * REACH, nu, gv, REACH)
    clear_dpre(d_v, r_v, ny, REACH, gv)
    for u in range(nu):
        for m in range(ny // 2):
            here = (u * ny // 2 + m) * LANES
            one = c_ref[0, :, here : here + LANES].astype(f32)
            two = c_ref[1, :, here : here + LANES].astype(f32)
            cot[2 * m, u], cot[2 * m + 1, u] = exchange_halves(one, two, left2)
    for copy in there:
        copy.wait_recv()
    parts = [got_h[u].astype(f32).reshape(ny, 1, sv, LANES) for u in range(rows)]
    vert[...] = jnp.concatenate(parts, axis=1).reshape(ny, nu * sv, LANES).astype(bf16)

    for t in range(0, 9, 2):
        last = min(t + 2, 9)
        got = dot_t(vert[...].reshape(ny * nu * sv, LANES), w_ref[1, t * LANES : last * LANES])
        for k in range(t, last):
            part = got[:, (k - t) * LANES : (k - t + 1) * LANES]
            for y in range(ny):
                here = (REACH + y) * (nu + 2) * gv + gv
                z_ref[k, here : here + nu * gv] = part[y * nu * sv : (y + 1) * nu * sv].reshape(
                    shape_v
                )

    def second_pass(y, carry):
        out = vert[y].astype(f32).reshape(shape_v)
        grad = cot[y].reshape(shape_v)
        for index, shift in enumerate(SHIFTS):
            place = place_of(y, shift, nu, shape_v, 0)
            p = preact_at(z_ref, y, nu, gv, shift, place, ny)
            sigma = sigma_of(p)
            keep = (place >= 0) & (place < ny)
            blend = b_ref[1, index : index + 1]
            out = out + blend * jnp.where(keep, p * sigma, 0.0)
            store_dpre(d_v, r_v, y + REACH, index, gv, keep, grad, blend, p, sigma)
        vout[y] = out.reshape(nu, sv, LANES)
        return carry

    lax.fori_loop(0, ny, second_pass, 0)
    gather_dpre(d_v, s_ref, ny, nu, gv, 0, ny)
    stacked = s_ref[: ny * nu * sv]
    grads = jnp.dot(stacked, w_ref[1], preferred_element_type=f32)
    dvert[...] = cot[...] + grads.reshape(dvert.shape)

    def block_back(to):
        block = dvert[:, pl.ds(to, 1)].reshape(ny, sv, LANES)
        low, high = jnp.swapaxes(block[:s], 0, 1), jnp.swapaxes(block[s:], 0, 1)
        both = jnp.concatenate(exchange_halves(low, high, left), axis=1)
        return both.astype(bf16)

    back = []
    for k in range(1, rows):
        to = lax.rem(row + k, rows)
        send_v[k - 1] = block_back(to)
        copy = remote(send_v.at[k - 1], got_v.at[row], back_sem, k - 1, (to, col))
        copy.start()
        back.append(copy)
    got_v[row] = block_back(row)
    pack_grads(vert[...].reshape(ny * nu * sv, LANES), stacked, r_v, payload, 1)
    sum_v.scatter()
    clear_dpre(d_h, r_h, nx, 2 * REACH, gh)
    for u in range(nu):
        for m in range(ny // 2):
            here = (u * ny // 2 + m) * LANES
            one, two = exchange_halves(vout[2 * m, u], vout[2 * m + 1, u], left2)
            o_ref[0, :, here : here + LANES] = one.astype(bf16)
            o_ref[1, :, here : here + LANES] = two.astype(bf16)
    for copy in back:
        copy.wait_recv()
    for r in range(rows):
        grad_h[:, r * 2 * s : (r + 1) * 2 * s] = got_v[r].astype(f32)

    def third_pass(x, carry):
        grad = grad_h[x].reshape(shape_h)
        for index, shift in enumerate(SHIFTS):
            place = place_of(x, shift, nv, shape_h, start)
            p = pre_ref[index, x]
            keep = (place >= 0) & (place < x_all)
            blend = b_ref[0, index : index + 1]
            store_dpre(
                d_h, r_h, x + 2 * REACH, index, gh, keep, grad, blend, p, sigma_of(p)
            )
        return carry

    lax.fori_loop(0, nx, third_pass, 0)
    sum_v.exchange()
    gather_dpre(d_h, s_ref, nx + 2 * REACH, nv, gh, start - REACH, x_all)
    stacked = s_ref[: (nx + 2 * REACH) * nvs]
    pack_grads(wide[...].reshape((nx + 2 * REACH) * nvs, LANES), stacked, r_h, payload, 0)
    sum_h.scatter()
    sum_v.gather()
    grads = jnp.dot(stacked, w_ref[0], preferred_element_type=f32)
    grads = grads.reshape(nx + 2 * REACH, nvs, LANES)
    rim_sent[0] = grads[:REACH].astype(bf16)
    rim_sent[1] = grads[nx + REACH :].astype(bf16)
    rims = [
        remote(rim_sent.at[0], rim_got.at[1], rim_sem, 0, (row, left_col)),
        remote(rim_sent.at[1], rim_got.at[0], rim_sem, 1, (row, right_col)),
    ]
    for copy in rims:
        copy.start()
    grad_h[...] += grads[REACH : REACH + nx]
    sum_h.exchange()
    for copy in rims:
        copy.wait_recv()

    @pl.when(col > 0)
    def _():
        grad_h[:REACH] += rim_got[0].astype(f32)

    @pl.when(col < cols - 1)
    def _():
        grad_h[nx - REACH :] += rim_got[1].astype(f32)

    sum_h.gather()
    for m in range(nv // 2):
        one = grad_h[:, 2 * m * s : (2 * m + 1) * s]
        two = grad_h[:, (2 * m + 1) * s : (2 * m + 2) * s]
        low, high = exchange_halves(one, two, left)
        lanes = slice(m * LANES, (m + 1) * LANES)
        dhor_ref[:s, :, lanes] = jnp.swapaxes(low, 0, 1).astype(bf16)
        dhor_ref[s:, :, lanes] = jnp.swapaxes(high, 0, 1).astype(bf16)
    factor = float(nu * ny * nv * x_all) ** (-0.5)
    sum_v.finish()
    unpack_grads(sum_ref, 1, shear_ref, gw_v_ref, gb_v_ref, factor)
    sum_h.finish()
    unpack_grads(sum_ref, 0, shear_ref, gw_h_ref, gb_h_ref, factor)
    for copy in halo + there + back + rims:
        copy.wait_send()


def per_device(features, weight_h, weight_v, beta_h, beta_v, shear_set, cotangent):
    rows, cols = lax.axis_size("vrow"), lax.axis_size("img")
    channels = weight_h.shape[0]
    u_local, y_all, x_local, merged = features.shape
    v_all = merged // channels
    v_local = v_all // rows
    u_all = u_local * rows
    s_h = u_local * y_all // 2
    s_v = v_local * x_local // 2
    f32, bf16 = jnp.float32, jnp.bfloat16
    count = len(SHIFTS)
    assert u_local == 1 and v_local == 2 and s_h % 8 == 0 and s_v % 8 == 0

    def tap_major(weight):
        return jnp.transpose(weight, (2, 3, 0, 1)).reshape(9, channels, channels)

    flat_h = (x_local, v_all * s_h, LANES)
    flat_v = (y_all, u_all * s_v, LANES)
    four_v = (y_all, u_all, s_v, LANES)
    rim = (REACH, v_all * s_h, LANES)
    grads = 5 * channels
    chunk = (grads // cols, LANES)
    gh, gv = s_h // 8, s_v // 8
    wide_x, wide_y = x_local + 2 * REACH, y_all + 2 * REACH
    products = max(wide_x * (v_all + 2) * gh, wide_y * (u_all + 2) * gv)
    vmem, dma = pltpu.VMEM, pltpu.SemaphoreType.DMA
    whole = pl.BlockSpec(memory_space=vmem)
    shape = jax.ShapeDtypeStruct
    output, dhor, gw_h, gw_v, gb_h, gb_v = pl.pallas_call(
        functools.partial(field_kernel, rows, cols),
        out_shape=[
            shape(cotangent.shape, bf16),
            shape(features.shape[1:], bf16),
            shape((9, channels, channels), f32),
            shape((9, channels, channels), f32),
            shape(beta_h.shape, f32),
            shape(beta_v.shape, f32),
        ],
        in_specs=[whole] * 5 + [pl.BlockSpec(memory_space=pltpu.SMEM), whole],
        out_specs=[whole] * 6,
        scratch_shapes=[
            vmem((wide_x,) + flat_h[1:], bf16),
            vmem((2, 9 * LANES, LANES), bf16),
            vmem((2, 8, LANES), f32),
            vmem((9, products, 8, LANES), f32),
            vmem((count, x_local, v_all * gh, 8, LANES), f32),
            vmem((x_local, v_all, s_h, LANES), f32),
            vmem((rows - 1, y_all * s_v, LANES), bf16),
            vmem((rows, y_all * s_v, LANES), bf16),
            vmem(flat_v, bf16),
            vmem(four_v, f32),
            vmem(four_v, f32),
            vmem(four_v, f32),
            vmem((rows - 1, x_local, 2 * s_h, LANES), bf16),
            vmem((rows, x_local, 2 * s_h, LANES), bf16),
            vmem(flat_h, f32),
            vmem((2,) + rim, bf16),
            vmem((2,) + rim, bf16),
            vmem((2, grads, LANES), f32),
            vmem((2, grads, LANES), f32),
            vmem((2, cols - 1) + chunk, f32),
            vmem((2, rows) + chunk, f32),
            vmem((max(wide_x * flat_h[1], y_all * flat_v[1]), 9 * LANES), bf16),
            vmem((count, x_local + 4 * REACH, (v_all + 2) * gh, 8, LANES), f32),
            vmem((count, wide_y, (u_all + 2) * gv, 8, LANES), f32),
            vmem((count, 8, LANES), f32),
            vmem((count, 8, LANES), f32),
            dma((2, 2)),
            dma((2, rows - 1)),
            dma((2, rows - 1)),
            dma((2, 2)),
            dma((2, 2, cols - 1)),
            dma((2, 2, rows - 1)),
            dma((2, 2, cols - 1)),
        ],
        compiler_params=pltpu.CompilerParams(
            collective_id=0, has_side_effects=True, vmem_limit_bytes=VMEM_LIMIT
        ),
        name="light_field",
    )(
        features.reshape(features.shape[1:]),
        tap_major(weight_h),
        tap_major(weight_v),
        beta_h,
        beta_v,
        shear_set,
        cotangent,
    )

    def tap_minor(grad):
        return jnp.transpose(grad.reshape(3, 3, channels, channels), (2, 3, 0, 1))

    return output, dhor.reshape(features.shape), tap_minor(gw_h), tap_minor(gw_v), gb_h, gb_v


def solution(mesh):
    placed = (P("vrow", None, "img", None), P(), P(), P(), P(), P(), P("vrow", "img", None))
    return jax.shard_map(
        per_device,
        mesh=mesh,
        in_specs=placed,
        out_specs=(P("vrow", "img", None), P("vrow", None, "img", None), P(), P(), P(), P()),
        check_vma=False,
    )
```

```python
import functools

import jax
import jax.numpy as jnp
from jax import lax
from jax.experimental import pallas as pl
from jax.experimental.pallas import tpu as pltpu
from jax.sharding import PartitionSpec as P

SHIFTS = (-2, -1, 0, 1, 2)
REACH = 3
TAPS = tuple((i, j) for i in (-1, 0, 1) for j in (-1, 0, 1))
LANES = 128
MESH = pl.DeviceIdType.MESH
VMEM_LIMIT = 60 * 1024 * 1024


def place_of(x, shift, views, shape, start, middle=None):
    middle = views // 2 if middle is None else middle
    view = lax.broadcasted_iota(jnp.int32, shape, 0) // (shape[0] // views) - middle
    return start + x - shift * view


def dot_t(x, y):
    return lax.dot_general(x, y, (((1,), (1,)), ((), ())), preferred_element_type=jnp.float32)


def tap_products(f_ref, w_ref, which, z_ref, views, first, length):
    rows = f_ref.shape[1]
    per = rows // 8
    step = per // views * (views + 2)
    source = f_ref[first : first + length].reshape(length * rows, LANES)
    for t in range(0, 9, 2):
        last = min(t + 2, 9)
        got = dot_t(source, w_ref[which, t * LANES : last * LANES])
        for k in range(t, last):
            part = got[:, (k - t) * LANES : (k - t + 1) * LANES]
            for x in range(length):
                here = (first + x) * step + per // views
                z_ref[k, here : here + per] = part[x * rows : (x + 1) * rows].reshape(
                    per, 8, LANES
                )


def clear_products(z_ref, columns, views, group, rim):
    step = (views + 2) * group
    side = jnp.zeros((9, group, 8, LANES), jnp.float32)

    def body(x, carry):
        z_ref[:, pl.ds(x * step, group)] = side
        z_ref[:, pl.ds(x * step + (views + 1) * group, group)] = side
        return carry

    lax.fori_loop(0, columns, body, 0)
    if rim:
        zero = jnp.zeros((9, rim * step, 8, LANES), jnp.float32)
        z_ref[:, : rim * step] = zero
        z_ref[:, (columns - rim) * step : columns * step] = zero


def preact_at(z_ref, x, views, group, shift, place, total, first=0, width=None):
    per = (views if width is None else width) * group
    step = (views + 2) * group
    sums = {}
    for t, (i, j) in enumerate(TAPS):
        here = (x + (REACH + j + shift * i)) * step + (1 + i + first) * group
        term = z_ref[t, pl.ds(here, per)]
        sums[j] = term if j not in sums else sums[j] + term
    low = jnp.where(place != 0, sums[-1], 0.0)
    high = jnp.where(place != total - 1, sums[1], 0.0)
    return sums[0] + low + high


def sigma_of(p):
    return 0.5 * jnp.tanh(0.5 * p) + 0.5


def store_dpre(d_ref, r_ref, x, index, group, keep, grad, blend, p, sigma):
    act = jnp.where(keep, p * sigma, 0.0)
    r_ref[index] += jnp.sum(grad * act, axis=0)
    slope = sigma * (1.0 + p * (1.0 - sigma))
    dpre = jnp.where(keep, blend * grad * slope, 0.0)
    d_ref[index, x, group : group + grad.shape[0]] = dpre


def clear_dpre(d_ref, r_ref, nx, pad, group):
    count, _, per, _, _ = d_ref.shape
    r_ref[...] = jnp.zeros_like(r_ref)
    rim = jnp.zeros((count, pad, per, 8, LANES), jnp.float32)
    d_ref[:, 0:pad] = rim
    d_ref[:, pad + nx : 2 * pad + nx] = rim
    side = jnp.zeros((count, nx, group, 8, LANES), jnp.float32)
    d_ref[:, pad : pad + nx, 0:group] = side
    d_ref[:, pad : pad + nx, per - group : per] = side


def gather_dpre(d_ref, s_ref, length, views, group, start, total):
    per = views * group

    def body(x, carry):
        sums = [None] * 9
        for index, shift in enumerate(SHIFTS):
            place = place_of(x, shift, views, (per, 8, LANES), start)
            inside = (place >= 0) & (place < total)
            for t, (i, j) in enumerate(TAPS):
                term = d_ref[
                    index, x + (REACH - j - shift * i), (1 - i) * group : (1 - i) * group + per
                ]
                if j != 0:
                    term = jnp.where(inside, term, 0.0)
                sums[t] = term if sums[t] is None else sums[t] + term
        here = pl.ds(pl.multiple_of(x * (per * 8), 16), per * 8)
        for t in range(9):
            s_ref[here, t * LANES : (t + 1) * LANES] = (
                sums[t].reshape(per * 8, LANES).astype(jnp.bfloat16)
            )
        return carry

    lax.fori_loop(0, length, body, 0)


def pack_grads(source, stacked, r_ref, out_ref, which):
    wide = lax.dot_general(
        source, stacked, (((0,), (0,)), ((), ())), preferred_element_type=jnp.float32
    )
    half = LANES // 2
    first, second = wide[:half], wide[half:]
    left = lax.broadcasted_iota(jnp.int32, (half, LANES), 1) < half
    sums = jnp.sum(r_ref[...], axis=1)
    sums = sums + pltpu.roll(sums, half, 1)
    for m in range(5):
        low = slice(2 * m * LANES, (2 * m + 1) * LANES)
        even = first[:, low] + pltpu.roll(second[:, low], half, 1)
        if m < 4:
            high = slice((2 * m + 1) * LANES, (2 * m + 2) * LANES)
            odd = pltpu.roll(first[:, high], half, 1) + second[:, high]
        else:
            odd = jnp.concatenate(
                [sums, jnp.zeros((half - sums.shape[0], LANES), jnp.float32)], axis=0
            )
        out_ref[which, m * half : (m + 1) * half] = jnp.where(left, even, odd)


def exchange_halves(one, two, left):
    return jnp.where(left, one, half_roll(two)), jnp.where(left, half_roll(one), two)


def stack_weights(weight_ref, w_ref, which, left):
    half = LANES // 2
    for t in range(9):
        tap = weight_ref[t].astype(jnp.float32)
        twice = jnp.concatenate([tap, tap], axis=1)
        both = jnp.concatenate(
            [jnp.where(left, twice, 0.0), jnp.where(left, 0.0, twice)], axis=0
        )
        w_ref[which, t * LANES : (t + 1) * LANES] = both.astype(jnp.bfloat16)


def stack_blends(beta_ref, shear_ref, b_ref, which):
    beta = beta_ref[...]
    beta = jnp.concatenate([beta, beta], axis=1)
    for index, shift in enumerate(SHIFTS):
        total = jnp.zeros((1, LANES), jnp.float32)
        for k in range(beta.shape[0]):
            total = total + jnp.where(shear_ref[k] == shift, 1.0, 0.0) * beta[k : k + 1]
        b_ref[which, index : index + 1] = total


def unpack_grads(sum_ref, which, shear_ref, weight_ref, beta_ref, factor):
    half = LANES // 2
    for m in range(5):
        tile = sum_ref[which, m * half : (m + 1) * half] * factor
        turned = jnp.transpose(tile)
        weight_ref[2 * m] = turned[:half]
        if m < 4:
            weight_ref[2 * m + 1] = turned[half:]
        else:
            raw = half_roll(tile[:8])[:, :half]
    for k in range(beta_ref.shape[0]):
        total = jnp.zeros((1, half), jnp.float32)
        for index, shift in enumerate(SHIFTS):
            total = total + jnp.where(shear_ref[k] == shift, 1.0, 0.0) * raw[index : index + 1]
        beta_ref[k : k + 1] = total


def half_roll(x):
    return pltpu.roll(x, LANES // 2, x.ndim - 1)


def remote(src, dst, sems, k, device):
    return pltpu.make_async_remote_copy(
        src_ref=src,
        dst_ref=dst,
        send_sem=sems.at[0, k],
        recv_sem=sems.at[1, k],
        device_id=device,
        device_id_type=MESH,
    )


class Sum:
    def __init__(self, rows, cols, x_ref, o_ref, heard, totals, sem_a, sem_b, sem_c):
        self.rows, self.cols = rows, cols
        self.x_ref, self.o_ref, self.heard, self.totals = x_ref, o_ref, heard, totals
        self.sems = (sem_a, sem_b, sem_c)
        self.row, self.col = lax.axis_index("vrow"), lax.axis_index("img")
        self.size = heard.shape[1]
        self.sent = []

    def chunk(self, index):
        return pl.ds(pl.multiple_of(index * self.size, 8), self.size)

    def scatter(self):
        self.first = []
        for k in range(1, self.cols):
            to = lax.rem(self.col + k, self.cols)
            source = self.x_ref.at[self.chunk(to)]
            copy = remote(source, self.heard.at[k - 1], self.sems[0], k - 1, (self.row, to))
            copy.start()
            self.first.append(copy)

    def exchange(self):
        total = self.x_ref[self.chunk(self.col)]
        for k, copy in enumerate(self.first):
            copy.wait_recv()
            total = total + self.heard[k]
        self.totals[self.row] = total
        self.second = []
        for k in range(1, self.rows):
            to = lax.rem(self.row + k, self.rows)
            mine = self.totals.at[self.row]
            copy = remote(mine, mine, self.sems[1], k - 1, (to, self.col))
            copy.start()
            self.second.append(copy)

    def gather(self):
        for copy in self.second:
            copy.wait_recv()
        total = self.totals[0]
        for k in range(1, self.rows):
            total = total + self.totals[k]
        self.o_ref[self.chunk(self.col)] = total
        self.third = []
        for k in range(1, self.cols):
            to = lax.rem(self.col + k, self.cols)
            mine = self.o_ref.at[self.chunk(self.col)]
            copy = remote(mine, mine, self.sems[2], k - 1, (self.row, to))
            copy.start()
            self.third.append(copy)

    def finish(self):
        for copy in self.third:
            copy.wait_recv()
        for copy in self.first + self.second + self.third:
            copy.wait_send()


def field_kernel(
    rows,
    cols,
    f_ref,
    weight_h_ref,
    weight_v_ref,
    beta_h_ref,
    beta_v_ref,
    shear_ref,
    c_ref,
    o_ref,
    dhor_ref,
    gw_h_ref,
    gw_v_ref,
    gb_h_ref,
    gb_v_ref,
    wide,
    w_ref,
    b_ref,
    z_ref,
    pre_ref,
    hfeat,
    send_h,
    got_h,
    vert,
    cot,
    vout,
    dvert,
    send_v,
    got_v,
    grad_h,
    rim_sent,
    rim_got,
    payload,
    sum_ref,
    heard,
    totals,
    s_ref,
    d_h,
    d_v,
    r_h,
    r_v,
    halo_sem,
    there_sem,
    back_sem,
    rim_sem,
    sum_a,
    sum_b,
    sum_c,
):
    row, col = lax.axis_index("vrow"), lax.axis_index("img")
    nx, nvs, _ = grad_h.shape
    ny, nu, sv, _ = dvert.shape
    s = f_ref.shape[0] // 2
    nv = nvs // s
    gh, gv = s // 8, sv // 8
    x_all = nx * cols
    start = col * nx
    f32, bf16 = jnp.float32, jnp.bfloat16
    shape_h, shape_v = (nv * gh, 8, LANES), (nu * gv, 8, LANES)
    left = lax.broadcasted_iota(jnp.int32, (1, 1, LANES), 2) < LANES // 2
    left2 = lax.broadcasted_iota(jnp.int32, (1, LANES), 1) < LANES // 2
    right_col, left_col = lax.rem(col + 1, cols), lax.rem(col + cols - 1, cols)

    barrier = pltpu.get_barrier_semaphore()
    for k in range(1, cols):
        peer = (row, lax.rem(col + k, cols))
        pl.semaphore_signal(barrier, inc=1, device_id=peer, device_id_type=MESH)
    for k in range(1, rows):
        peer = (lax.rem(row + k, rows), col)
        pl.semaphore_signal(barrier, inc=1, device_id=peer, device_id_type=MESH)

    for m in range(nv // 2):
        block = f_ref[:, :, m * LANES : (m + 1) * LANES].astype(f32)
        low, high = jnp.swapaxes(block[:s], 0, 1), jnp.swapaxes(block[s:], 0, 1)
        both = jnp.concatenate(exchange_halves(low, high, left), axis=1)
        wide[REACH : REACH + nx, m * 2 * s : (m + 1) * 2 * s] = both.astype(bf16)
    pl.semaphore_wait(barrier, cols + rows - 2)

    halo = [
        remote(
            wide.at[pl.ds(nx, REACH)],
            wide.at[pl.ds(0, REACH)],
            halo_sem,
            0,
            (row, right_col),
        ),
        remote(
            wide.at[pl.ds(REACH, REACH)],
            wide.at[pl.ds(nx + REACH, REACH)],
            halo_sem,
            1,
            (row, left_col),
        ),
    ]
    for copy in halo:
        copy.start()
    stack_weights(weight_h_ref, w_ref, 0, left2)
    stack_blends(beta_h_ref, shear_ref, b_ref, 0)
    clear_products(z_ref, nx + 2 * REACH, nv, gh, 0)
    tap_products(wide, w_ref, 0, z_ref, nv, REACH, nx)
    for copy in halo:
        copy.wait_recv()

    @pl.when(col == 0)
    def _():
        wide[:REACH] = jnp.zeros((REACH, nvs, LANES), bf16)

    @pl.when(col == cols - 1)
    def _():
        wide[nx + REACH :] = jnp.zeros((REACH, nvs, LANES), bf16)

    tap_products(wide, w_ref, 0, z_ref, nv, 0, REACH)
    tap_products(wide, w_ref, 0, z_ref, nv, nx + REACH, REACH)

    shape_two = (2 * gh, 8, LANES)
    unroll = 4 if nx % 4 == 0 else 1

    def first_pass(to):
        rows_two = pl.ds(pl.multiple_of(to * (2 * s), 16), 2 * s)

        def column(x):
            out = wide[x + REACH, rows_two].astype(f32).reshape(shape_two)
            for index, shift in enumerate(SHIFTS):
                place = place_of(x, shift, 2, shape_two, start, nv // 2 - 2 * to)
                p = preact_at(z_ref, x, nv, gh, shift, place, x_all, 2 * to, 2)
                pre_ref[index, x, pl.ds(2 * to * gh, 2 * gh)] = p
                keep = (place >= 0) & (place < x_all)
                out = out + b_ref[0, index : index + 1] * jnp.where(keep, p * sigma_of(p), 0.0)
            hfeat[x] = out.reshape(2, s, LANES)

        def body(step, carry):
            for k in range(unroll):
                column(step * unroll + k)
            return carry

        lax.fori_loop(0, nx // unroll, body, 0)
        low, high = exchange_halves(hfeat[:, 0], hfeat[:, 1], left)
        both = [jnp.swapaxes(low, 0, 1), jnp.swapaxes(high, 0, 1)]
        return jnp.concatenate(both, axis=0).reshape(ny * sv, LANES).astype(bf16)

    there = []
    for k in range(1, rows):
        to = lax.rem(row + k, rows)
        send_h[k - 1] = first_pass(to)
        copy = remote(send_h.at[k - 1], got_h.at[row], there_sem, k - 1, (to, col))
        copy.start()
        there.append(copy)
    got_h[row] = first_pass(row)

    sum_h, sum_v = [
        Sum(
            rows,
            cols,
            payload.at[n],
            sum_ref.at[n],
            heard.at[n],
            totals.at[n],
            sum_a.at[n],
            sum_b.at[n],
            sum_c.at[n],
        )
        for n in range(2)
    ]
    stack_weights(weight_v_ref, w_ref, 1, left2)
    stack_blends(beta_v_ref, shear_ref, b_ref, 1)
    clear_products(z_ref, ny + 2 * REACH, nu, gv, REACH)
    clear_dpre(d_v, r_v, ny, REACH, gv)
    for u in range(nu):
        for m in range(ny // 2):
            here = (u * ny // 2 + m) * LANES
            one = c_ref[0, :, here : here + LANES].astype(f32)
            two = c_ref[1, :, here : here + LANES].astype(f32)
            cot[2 * m, u], cot[2 * m + 1, u] = exchange_halves(one, two, left2)
    for copy in there:
        copy.wait_recv()
    parts = [got_h[u].astype(f32).reshape(ny, 1, sv, LANES) for u in range(rows)]
    vert[...] = jnp.concatenate(parts, axis=1).reshape(ny, nu * sv, LANES).astype(bf16)

    for t in range(0, 9, 2):
        last = min(t + 2, 9)
        got = dot_t(vert[...].reshape(ny * nu * sv, LANES), w_ref[1, t * LANES : last * LANES])
        for k in range(t, last):
            part = got[:, (k - t) * LANES : (k - t + 1) * LANES]
            for y in range(ny):
                here = (REACH + y) * (nu + 2) * gv + gv
                z_ref[k, here : here + nu * gv] = part[y * nu * sv : (y + 1) * nu * sv].reshape(
                    shape_v
                )

    def second_pass(y, carry):
        out = vert[y].astype(f32).reshape(shape_v)
        grad = cot[y].reshape(shape_v)
        for index, shift in enumerate(SHIFTS):
            place = place_of(y, shift, nu, shape_v, 0)
            p = preact_at(z_ref, y, nu, gv, shift, place, ny)
            sigma = sigma_of(p)
            keep = (place >= 0) & (place < ny)
            blend = b_ref[1, index : index + 1]
            out = out + blend * jnp.where(keep, p * sigma, 0.0)
            store_dpre(d_v, r_v, y + REACH, index, gv, keep, grad, blend, p, sigma)
        vout[y] = out.reshape(nu, sv, LANES)
        return carry

    lax.fori_loop(0, ny, second_pass, 0)
    gather_dpre(d_v, s_ref, ny, nu, gv, 0, ny)
    stacked = s_ref[: ny * nu * sv]
    grads = jnp.dot(stacked, w_ref[1], preferred_element_type=f32)
    dvert[...] = cot[...] + grads.reshape(dvert.shape)

    def block_back(to):
        block = dvert[:, pl.ds(to, 1)].reshape(ny, sv, LANES)
        low, high = jnp.swapaxes(block[:s], 0, 1), jnp.swapaxes(block[s:], 0, 1)
        both = jnp.concatenate(exchange_halves(low, high, left), axis=1)
        return both.astype(bf16)

    back = []
    for k in range(1, rows):
        to = lax.rem(row + k, rows)
        send_v[k - 1] = block_back(to)
        copy = remote(send_v.at[k - 1], got_v.at[row], back_sem, k - 1, (to, col))
        copy.start()
        back.append(copy)
    got_v[row] = block_back(row)
    pack_grads(vert[...].reshape(ny * nu * sv, LANES), stacked, r_v, payload, 1)
    sum_v.scatter()
    clear_dpre(d_h, r_h, nx, 2 * REACH, gh)
    for u in range(nu):
        for m in range(ny // 2):
            here = (u * ny // 2 + m) * LANES
            one, two = exchange_halves(vout[2 * m, u], vout[2 * m + 1, u], left2)
            o_ref[0, :, here : here + LANES] = one.astype(bf16)
            o_ref[1, :, here : here + LANES] = two.astype(bf16)
    for copy in back:
        copy.wait_recv()
    for r in range(rows):
        grad_h[:, r * 2 * s : (r + 1) * 2 * s] = got_v[r].astype(f32)
    sum_v.exchange()

    def third_pass(x, carry):
        grad = grad_h[x].reshape(shape_h)
        for index, shift in enumerate(SHIFTS):
            place = place_of(x, shift, nv, shape_h, start)
            p = pre_ref[index, x]
            keep = (place >= 0) & (place < x_all)
            blend = b_ref[0, index : index + 1]
            store_dpre(
                d_h, r_h, x + 2 * REACH, index, gh, keep, grad, blend, p, sigma_of(p)
            )
        return carry

    lax.fori_loop(0, nx, third_pass, 0)
    sum_v.gather()
    gather_dpre(d_h, s_ref, nx + 2 * REACH, nv, gh, start - REACH, x_all)
    stacked = s_ref[: (nx + 2 * REACH) * nvs]
    pack_grads(wide[...].reshape((nx + 2 * REACH) * nvs, LANES), stacked, r_h, payload, 0)
    sum_h.scatter()
    grads = jnp.dot(stacked, w_ref[0], preferred_element_type=f32)
    grads = grads.reshape(nx + 2 * REACH, nvs, LANES)
    rim_sent[0] = grads[:REACH].astype(bf16)
    rim_sent[1] = grads[nx + REACH :].astype(bf16)
    rims = [
        remote(rim_sent.at[0], rim_got.at[1], rim_sem, 0, (row, left_col)),
        remote(rim_sent.at[1], rim_got.at[0], rim_sem, 1, (row, right_col)),
    ]
    for copy in rims:
        copy.start()
    grad_h[...] += grads[REACH : REACH + nx]
    sum_h.exchange()
    factor = float(nu * ny * nv * x_all) ** (-0.5)
    sum_v.finish()
    unpack_grads(sum_ref, 1, shear_ref, gw_v_ref, gb_v_ref, factor)
    for copy in rims:
        copy.wait_recv()

    @pl.when(col > 0)
    def _():
        grad_h[:REACH] += rim_got[0].astype(f32)

    @pl.when(col < cols - 1)
    def _():
        grad_h[nx - REACH :] += rim_got[1].astype(f32)

    sum_h.gather()
    for m in range(nv // 2):
        one = grad_h[:, 2 * m * s : (2 * m + 1) * s]
        two = grad_h[:, (2 * m + 1) * s : (2 * m + 2) * s]
        low, high = exchange_halves(one, two, left)
        lanes = slice(m * LANES, (m + 1) * LANES)
        dhor_ref[:s, :, lanes] = jnp.swapaxes(low, 0, 1).astype(bf16)
        dhor_ref[s:, :, lanes] = jnp.swapaxes(high, 0, 1).astype(bf16)
    sum_h.finish()
    unpack_grads(sum_ref, 0, shear_ref, gw_h_ref, gb_h_ref, factor)
    for copy in halo + there + back + rims:
        copy.wait_send()


def hand_out_kernel(*refs):
    count = len(refs) // 2
    copies = [
        pltpu.make_async_copy(refs[k], refs[count + k], refs[-1].at[k]) for k in range(count)
    ]
    for copy in copies:
        copy.start()
    for copy in copies:
        copy.wait()


def hand_out(*arrays):
    anywhere = pl.BlockSpec(memory_space=pl.ANY)
    return pl.pallas_call(
        hand_out_kernel,
        out_shape=[jax.ShapeDtypeStruct(a.shape, a.dtype) for a in arrays],
        in_specs=[anywhere] * len(arrays),
        out_specs=[anywhere] * len(arrays),
        scratch_shapes=[pltpu.SemaphoreType.DMA((len(arrays),))],
        compiler_params=pltpu.CompilerParams(vmem_limit_bytes=VMEM_LIMIT),
        name="hand_out",
    )(*arrays)


def per_device(features, weight_h, weight_v, beta_h, beta_v, shear_set, cotangent):
    rows, cols = lax.axis_size("vrow"), lax.axis_size("img")
    channels = weight_h.shape[0]
    u_local, y_all, x_local, merged = features.shape
    v_all = merged // channels
    v_local = v_all // rows
    u_all = u_local * rows
    s_h = u_local * y_all // 2
    s_v = v_local * x_local // 2
    f32, bf16 = jnp.float32, jnp.bfloat16
    count = len(SHIFTS)
    assert u_local == 1 and v_local == 2 and s_h % 8 == 0 and s_v % 8 == 0

    def tap_major(weight):
        return jnp.transpose(weight, (2, 3, 0, 1)).reshape(9, channels, channels)

    flat_h = (x_local, v_all * s_h, LANES)
    flat_v = (y_all, u_all * s_v, LANES)
    four_v = (y_all, u_all, s_v, LANES)
    rim = (REACH, v_all * s_h, LANES)
    grads = 5 * channels
    chunk = (grads // cols, LANES)
    gh, gv = s_h // 8, s_v // 8
    wide_x, wide_y = x_local + 2 * REACH, y_all + 2 * REACH
    products = max(wide_x * (v_all + 2) * gh, wide_y * (u_all + 2) * gv)
    vmem, dma = pltpu.VMEM, pltpu.SemaphoreType.DMA
    whole = pl.BlockSpec(memory_space=vmem)
    shape = jax.ShapeDtypeStruct
    results = pl.pallas_call(
        functools.partial(field_kernel, rows, cols),
        out_shape=[
            shape(cotangent.shape, bf16),
            shape(features.shape[1:], bf16),
            shape((9, channels, channels), f32),
            shape((9, channels, channels), f32),
            shape(beta_h.shape, f32),
            shape(beta_v.shape, f32),
        ],
        in_specs=[whole] * 5 + [pl.BlockSpec(memory_space=pltpu.SMEM), whole],
        out_specs=[whole] * 6,
        scratch_shapes=[
            vmem((wide_x,) + flat_h[1:], bf16),
            vmem((2, 9 * LANES, LANES), bf16),
            vmem((2, 8, LANES), f32),
            vmem((9, products, 8, LANES), f32),
            vmem((count, x_local, v_all * gh, 8, LANES), f32),
            vmem((x_local, 2, s_h, LANES), f32),
            vmem((rows - 1, y_all * s_v, LANES), bf16),
            vmem((rows, y_all * s_v, LANES), bf16),
            vmem(flat_v, bf16),
            vmem(four_v, f32),
            vmem(four_v, f32),
            vmem(four_v, f32),
            vmem((rows - 1, x_local, 2 * s_h, LANES), bf16),
            vmem((rows, x_local, 2 * s_h, LANES), bf16),
            vmem(flat_h, f32),
            vmem((2,) + rim, bf16),
            vmem((2,) + rim, bf16),
            vmem((2, grads, LANES), f32),
            vmem((2, grads, LANES), f32),
            vmem((2, cols - 1) + chunk, f32),
            vmem((2, rows) + chunk, f32),
            vmem((max(wide_x * flat_h[1], y_all * flat_v[1]), 9 * LANES), bf16),
            vmem((count, x_local + 4 * REACH, (v_all + 2) * gh, 8, LANES), f32),
            vmem((count, wide_y, (u_all + 2) * gv, 8, LANES), f32),
            vmem((count, 8, LANES), f32),
            vmem((count, 8, LANES), f32),
            dma((2, 2)),
            dma((2, rows - 1)),
            dma((2, rows - 1)),
            dma((2, 2)),
            dma((2, 2, cols - 1)),
            dma((2, 2, rows - 1)),
            dma((2, 2, cols - 1)),
        ],
        compiler_params=pltpu.CompilerParams(
            collective_id=0, has_side_effects=True, vmem_limit_bytes=VMEM_LIMIT
        ),
        name="light_field",
    )(
        features.reshape(features.shape[1:]),
        tap_major(weight_h),
        tap_major(weight_v),
        beta_h,
        beta_v,
        shear_set,
        cotangent,
    )

    output, dhor, gw_h, gw_v, gb_h, gb_v = hand_out(*results)

    def tap_minor(grad):
        return jnp.transpose(grad.reshape(3, 3, channels, channels), (2, 3, 0, 1))

    return output, dhor.reshape(features.shape), tap_minor(gw_h), tap_minor(gw_v), gb_h, gb_v


def solution(mesh):
    placed = (P("vrow", None, "img", None), P(), P(), P(), P(), P(), P("vrow", "img", None))
    return jax.shard_map(
        per_device,
        mesh=mesh,
        in_specs=placed,
        out_specs=(P("vrow", "img", None), P("vrow", None, "img", None), P(), P(), P(), P()),
        check_vma=False,
    )
```

```python
import functools

import jax
import jax.numpy as jnp
from jax import lax
from jax.experimental import pallas as pl
from jax.experimental.pallas import tpu as pltpu
from jax.sharding import PartitionSpec as P

SHIFTS = (-2, -1, 0, 1, 2)
REACH = 3
TAPS = tuple((i, j) for i in (-1, 0, 1) for j in (-1, 0, 1))
LANES = 128
MESH = pl.DeviceIdType.MESH
VMEM_LIMIT = 60 * 1024 * 1024


def place_of(x, shift, views, shape, start):
    view = lax.broadcasted_iota(jnp.int32, shape, 0) // (shape[0] // views) - views // 2
    return start + x - shift * view


def dot_t(x, y):
    return lax.dot_general(x, y, (((1,), (1,)), ((), ())), preferred_element_type=jnp.float32)


def tap_products(f_ref, w_ref, which, z_ref, views, first, length):
    rows = f_ref.shape[1]
    per = rows // 8
    step = per // views * (views + 2)
    source = f_ref[first : first + length].reshape(length * rows, LANES)
    for t in range(0, 9, 2):
        last = min(t + 2, 9)
        got = dot_t(source, w_ref[which, t * LANES : last * LANES])
        for k in range(t, last):
            part = got[:, (k - t) * LANES : (k - t + 1) * LANES]
            for x in range(length):
                here = (first + x) * step + per // views
                z_ref[k, here : here + per] = part[x * rows : (x + 1) * rows].reshape(
                    per, 8, LANES
                )


def clear_products(z_ref, columns, views, group, rim):
    step = (views + 2) * group
    side = jnp.zeros((9, group, 8, LANES), jnp.float32)

    def body(x, carry):
        z_ref[:, pl.ds(x * step, group)] = side
        z_ref[:, pl.ds(x * step + (views + 1) * group, group)] = side
        return carry

    lax.fori_loop(0, columns, body, 0)
    if rim:
        zero = jnp.zeros((9, rim * step, 8, LANES), jnp.float32)
        z_ref[:, : rim * step] = zero
        z_ref[:, (columns - rim) * step : columns * step] = zero


def preact_at(z_ref, x, views, group, shift, place, total):
    step = (views + 2) * group
    sums = {}
    for t, (i, j) in enumerate(TAPS):
        here = (x + (REACH + j + shift * i)) * step + (1 + i) * group
        term = z_ref[t, pl.ds(here, views * group)]
        sums[j] = term if j not in sums else sums[j] + term
    low = jnp.where(place != 0, sums[-1], 0.0)
    high = jnp.where(place != total - 1, sums[1], 0.0)
    return sums[0] + low + high


def sigma_of(p):
    return 0.5 * jnp.tanh(0.5 * p) + 0.5


def store_dpre(d_ref, r_ref, x, index, group, keep, grad, blend, p, sigma):
    act = jnp.where(keep, p * sigma, 0.0)
    r_ref[index] += jnp.sum(grad * act, axis=0)
    slope = sigma * (1.0 + p * (1.0 - sigma))
    dpre = jnp.where(keep, blend * grad * slope, 0.0)
    d_ref[index, x, group : group + grad.shape[0]] = dpre


def clear_dpre(d_ref, r_ref, nx, pad, group):
    count, _, per, _, _ = d_ref.shape
    r_ref[...] = jnp.zeros_like(r_ref)
    rim = jnp.zeros((count, pad, per, 8, LANES), jnp.float32)
    d_ref[:, 0:pad] = rim
    d_ref[:, pad + nx : 2 * pad + nx] = rim
    side = jnp.zeros((count, nx, group, 8, LANES), jnp.float32)
    d_ref[:, pad : pad + nx, 0:group] = side
    d_ref[:, pad : pad + nx, per - group : per] = side


def gather_dpre(d_ref, s_ref, length, views, group, start, total):
    per = views * group

    def body(x, carry):
        sums = [None] * 9
        for index, shift in enumerate(SHIFTS):
            place = place_of(x, shift, views, (per, 8, LANES), start)
            inside = (place >= 0) & (place < total)
            for t, (i, j) in enumerate(TAPS):
                term = d_ref[
                    index, x + (REACH - j - shift * i), (1 - i) * group : (1 - i) * group + per
                ]
                if j != 0:
                    term = jnp.where(inside, term, 0.0)
                sums[t] = term if sums[t] is None else sums[t] + term
        here = pl.ds(pl.multiple_of(x * (per * 8), 16), per * 8)
        for t in range(9):
            s_ref[here, t * LANES : (t + 1) * LANES] = (
                sums[t].reshape(per * 8, LANES).astype(jnp.bfloat16)
            )
        return carry

    lax.fori_loop(0, length, body, 0)


def pack_grads(source, stacked, r_ref, out_ref, which):
    wide = lax.dot_general(
        source, stacked, (((0,), (0,)), ((), ())), preferred_element_type=jnp.float32
    )
    half = LANES // 2
    first, second = wide[:half], wide[half:]
    left = lax.broadcasted_iota(jnp.int32, (half, LANES), 1) < half
    sums = jnp.sum(r_ref[...], axis=1)
    sums = sums + pltpu.roll(sums, half, 1)
    for m in range(5):
        low = slice(2 * m * LANES, (2 * m + 1) * LANES)
        even = first[:, low] + pltpu.roll(second[:, low], half, 1)
        if m < 4:
            high = slice((2 * m + 1) * LANES, (2 * m + 2) * LANES)
            odd = pltpu.roll(first[:, high], half, 1) + second[:, high]
        else:
            odd = jnp.concatenate(
                [sums, jnp.zeros((half - sums.shape[0], LANES), jnp.float32)], axis=0
            )
        out_ref[which, m * half : (m + 1) * half] = jnp.where(left, even, odd)


def exchange_halves(one, two, left):
    return jnp.where(left, one, half_roll(two)), jnp.where(left, half_roll(one), two)


def stack_weights(weight_ref, w_ref, which, left):
    half = LANES // 2
    for t in range(9):
        tap = weight_ref[t].astype(jnp.float32)
        twice = jnp.concatenate([tap, tap], axis=1)
        both = jnp.concatenate(
            [jnp.where(left, twice, 0.0), jnp.where(left, 0.0, twice)], axis=0
        )
        w_ref[which, t * LANES : (t + 1) * LANES] = both.astype(jnp.bfloat16)


def stack_blends(beta_ref, shear_ref, b_ref, which):
    beta = beta_ref[...]
    beta = jnp.concatenate([beta, beta], axis=1)
    for index, shift in enumerate(SHIFTS):
        total = jnp.zeros((1, LANES), jnp.float32)
        for k in range(beta.shape[0]):
            total = total + jnp.where(shear_ref[k] == shift, 1.0, 0.0) * beta[k : k + 1]
        b_ref[which, index : index + 1] = total


def unpack_grads(sum_ref, which, shear_ref, weight_ref, beta_ref, factor):
    half = LANES // 2
    for m in range(5):
        tile = sum_ref[which, m * half : (m + 1) * half] * factor
        turned = jnp.transpose(tile)
        weight_ref[2 * m] = turned[:half]
        if m < 4:
            weight_ref[2 * m + 1] = turned[half:]
        else:
            raw = half_roll(tile[:8])[:, :half]
    for k in range(beta_ref.shape[0]):
        total = jnp.zeros((1, half), jnp.float32)
        for index, shift in enumerate(SHIFTS):
            total = total + jnp.where(shear_ref[k] == shift, 1.0, 0.0) * raw[index : index + 1]
        beta_ref[k : k + 1] = total


def half_roll(x):
    return pltpu.roll(x, LANES // 2, x.ndim - 1)


def remote(src, dst, sems, k, device):
    return pltpu.make_async_remote_copy(
        src_ref=src,
        dst_ref=dst,
        send_sem=sems.at[0, k],
        recv_sem=sems.at[1, k],
        device_id=device,
        device_id_type=MESH,
    )


class Sum:
    def __init__(self, rows, cols, x_ref, o_ref, heard, totals, sem_a, sem_b, sem_c):
        self.rows, self.cols = rows, cols
        self.x_ref, self.o_ref, self.heard, self.totals = x_ref, o_ref, heard, totals
        self.sems = (sem_a, sem_b, sem_c)
        self.row, self.col = lax.axis_index("vrow"), lax.axis_index("img")
        self.size = heard.shape[1]
        self.sent = []

    def chunk(self, index):
        return pl.ds(pl.multiple_of(index * self.size, 8), self.size)

    def scatter(self):
        self.first = []
        for k in range(1, self.cols):
            to = lax.rem(self.col + k, self.cols)
            source = self.x_ref.at[self.chunk(to)]
            copy = remote(source, self.heard.at[k - 1], self.sems[0], k - 1, (self.row, to))
            copy.start()
            self.first.append(copy)

    def exchange(self):
        total = self.x_ref[self.chunk(self.col)]
        for k, copy in enumerate(self.first):
            copy.wait_recv()
            total = total + self.heard[k]
        self.totals[self.row] = total
        self.second = []
        for k in range(1, self.rows):
            to = lax.rem(self.row + k, self.rows)
            mine = self.totals.at[self.row]
            copy = remote(mine, mine, self.sems[1], k - 1, (to, self.col))
            copy.start()
            self.second.append(copy)

    def gather(self):
        for copy in self.second:
            copy.wait_recv()
        total = self.totals[0]
        for k in range(1, self.rows):
            total = total + self.totals[k]
        self.o_ref[self.chunk(self.col)] = total
        self.third = []
        for k in range(1, self.cols):
            to = lax.rem(self.col + k, self.cols)
            mine = self.o_ref.at[self.chunk(self.col)]
            copy = remote(mine, mine, self.sems[2], k - 1, (self.row, to))
            copy.start()
            self.third.append(copy)

    def finish(self):
        for copy in self.third:
            copy.wait_recv()
        for copy in self.first + self.second + self.third:
            copy.wait_send()


def field_kernel(
    rows,
    cols,
    f_ref,
    weight_h_ref,
    weight_v_ref,
    beta_h_ref,
    beta_v_ref,
    shear_ref,
    c_ref,
    o_ref,
    dhor_ref,
    gw_h_ref,
    gw_v_ref,
    gb_h_ref,
    gb_v_ref,
    wide,
    w_ref,
    b_ref,
    z_ref,
    pre_ref,
    hfeat,
    send_h,
    got_h,
    vert,
    cot,
    vout,
    dvert,
    send_v,
    got_v,
    grad_h,
    rim_sent,
    rim_got,
    payload,
    sum_ref,
    heard,
    totals,
    s_ref,
    d_h,
    d_v,
    r_h,
    r_v,
    halo_sem,
    there_sem,
    back_sem,
    rim_sem,
    sum_a,
    sum_b,
    sum_c,
):
    row, col = lax.axis_index("vrow"), lax.axis_index("img")
    nx, nvs, _ = grad_h.shape
    ny, nu, sv, _ = dvert.shape
    s = f_ref.shape[0] // 2
    nv = nvs // s
    gh, gv = s // 8, sv // 8
    x_all = nx * cols
    start = col * nx
    f32, bf16 = jnp.float32, jnp.bfloat16
    shape_h, shape_v = (nv * gh, 8, LANES), (nu * gv, 8, LANES)
    left = lax.broadcasted_iota(jnp.int32, (1, 1, LANES), 2) < LANES // 2
    left2 = lax.broadcasted_iota(jnp.int32, (1, LANES), 1) < LANES // 2
    right_col, left_col = lax.rem(col + 1, cols), lax.rem(col + cols - 1, cols)

    barrier = pltpu.get_barrier_semaphore()
    for k in range(1, cols):
        peer = (row, lax.rem(col + k, cols))
        pl.semaphore_signal(barrier, inc=1, device_id=peer, device_id_type=MESH)
    for k in range(1, rows):
        peer = (lax.rem(row + k, rows), col)
        pl.semaphore_signal(barrier, inc=1, device_id=peer, device_id_type=MESH)

    for m in range(nv // 2):
        block = f_ref[:, :, m * LANES : (m + 1) * LANES].astype(f32)
        low, high = jnp.swapaxes(block[:s], 0, 1), jnp.swapaxes(block[s:], 0, 1)
        both = jnp.concatenate(exchange_halves(low, high, left), axis=1)
        wide[REACH : REACH + nx, m * 2 * s : (m + 1) * 2 * s] = both.astype(bf16)
    pl.semaphore_wait(barrier, cols + rows - 2)

    halo = [
        remote(
            wide.at[pl.ds(nx, REACH)],
            wide.at[pl.ds(0, REACH)],
            halo_sem,
            0,
            (row, right_col),
        ),
        remote(
            wide.at[pl.ds(REACH, REACH)],
            wide.at[pl.ds(nx + REACH, REACH)],
            halo_sem,
            1,
            (row, left_col),
        ),
    ]
    for copy in halo:
        copy.start()
    stack_weights(weight_h_ref, w_ref, 0, left2)
    stack_blends(beta_h_ref, shear_ref, b_ref, 0)
    clear_products(z_ref, nx + 2 * REACH, nv, gh, 0)
    tap_products(wide, w_ref, 0, z_ref, nv, REACH, nx)
    for copy in halo:
        copy.wait_recv()

    @pl.when(col == 0)
    def _():
        wide[:REACH] = jnp.zeros((REACH, nvs, LANES), bf16)

    @pl.when(col == cols - 1)
    def _():
        wide[nx + REACH :] = jnp.zeros((REACH, nvs, LANES), bf16)

    tap_products(wide, w_ref, 0, z_ref, nv, 0, REACH)
    tap_products(wide, w_ref, 0, z_ref, nv, nx + REACH, REACH)

    def first_pass(x, carry):
        out = wide[x + REACH].astype(f32).reshape(shape_h)
        for index, shift in enumerate(SHIFTS):
            place = place_of(x, shift, nv, shape_h, start)
            p = preact_at(z_ref, x, nv, gh, shift, place, x_all)
            pre_ref[index, x] = p
            keep = (place >= 0) & (place < x_all)
            out = out + b_ref[0, index : index + 1] * jnp.where(keep, p * sigma_of(p), 0.0)
        hfeat[x] = out.reshape(nv, s, LANES)
        return carry

    lax.fori_loop(0, nx, first_pass, 0)

    def block_there(to):
        views = hfeat[:, pl.ds(2 * to, 2)]
        low, high = exchange_halves(views[:, 0], views[:, 1], left)
        both = [jnp.swapaxes(low, 0, 1), jnp.swapaxes(high, 0, 1)]
        return jnp.concatenate(both, axis=0).reshape(ny * sv, LANES).astype(bf16)

    there = []
    for k in range(1, rows):
        to = lax.rem(row + k, rows)
        send_h[k - 1] = block_there(to)
        copy = remote(send_h.at[k - 1], got_h.at[row], there_sem, k - 1, (to, col))
        copy.start()
        there.append(copy)
    got_h[row] = block_there(row)

    sum_h, sum_v = [
        Sum(
            rows,
            cols,
            payload.at[n],
            sum_ref.at[n],
            heard.at[n],
            totals.at[n],
            sum_a.at[n],
            sum_b.at[n],
            sum_c.at[n],
        )
        for n in range(2)
    ]
    stack_weights(weight_v_ref, w_ref, 1, left2)
    stack_blends(beta_v_ref, shear_ref, b_ref, 1)
    clear_products(z_ref, ny + 2 * REACH, nu, gv, REACH)
    clear_dpre(d_v, r_v, ny, REACH, gv)
    for u in range(nu):
        for m in range(ny // 2):
            here = (u * ny // 2 + m) * LANES
            one = c_ref[0, :, here : here + LANES].astype(f32)
            two = c_ref[1, :, here : here + LANES].astype(f32)
            cot[2 * m, u], cot[2 * m + 1, u] = exchange_halves(one, two, left2)
    for copy in there:
        copy.wait_recv()
    parts = [got_h[u].astype(f32).reshape(ny, 1, sv, LANES) for u in range(rows)]
    vert[...] = jnp.concatenate(parts, axis=1).reshape(ny, nu * sv, LANES).astype(bf16)

    for t in range(0, 9, 2):
        last = min(t + 2, 9)
        got = dot_t(vert[...].reshape(ny * nu * sv, LANES), w_ref[1, t * LANES : last * LANES])
        for k in range(t, last):
            part = got[:, (k - t) * LANES : (k - t + 1) * LANES]
            for y in range(ny):
                here = (REACH + y) * (nu + 2) * gv + gv
                z_ref[k, here : here + nu * gv] = part[y * nu * sv : (y + 1) * nu * sv].reshape(
                    shape_v
                )

    def second_pass(y, carry):
        out = vert[y].astype(f32).reshape(shape_v)
        grad = cot[y].reshape(shape_v)
        for index, shift in enumerate(SHIFTS):
            place = place_of(y, shift, nu, shape_v, 0)
            p = preact_at(z_ref, y, nu, gv, shift, place, ny)
            sigma = sigma_of(p)
            keep = (place >= 0) & (place < ny)
            blend = b_ref[1, index : index + 1]
            out = out + blend * jnp.where(keep, p * sigma, 0.0)
            store_dpre(d_v, r_v, y + REACH, index, gv, keep, grad, blend, p, sigma)
        vout[y] = out.reshape(nu, sv, LANES)
        return carry

    lax.fori_loop(0, ny, second_pass, 0)
    gather_dpre(d_v, s_ref, ny, nu, gv, 0, ny)
    stacked = s_ref[: ny * nu * sv]
    grads = jnp.dot(stacked, w_ref[1], preferred_element_type=f32)
    dvert[...] = cot[...] + grads.reshape(dvert.shape)

    def block_back(to):
        block = dvert[:, pl.ds(to, 1)].reshape(ny, sv, LANES)
        low, high = jnp.swapaxes(block[:s], 0, 1), jnp.swapaxes(block[s:], 0, 1)
        both = jnp.concatenate(exchange_halves(low, high, left), axis=1)
        return both.astype(bf16)

    back = []
    for k in range(1, rows):
        to = lax.rem(row + k, rows)
        send_v[k - 1] = block_back(to)
        copy = remote(send_v.at[k - 1], got_v.at[row], back_sem, k - 1, (to, col))
        copy.start()
        back.append(copy)
    got_v[row] = block_back(row)
    pack_grads(vert[...].reshape(ny * nu * sv, LANES), stacked, r_v, payload, 1)
    sum_v.scatter()
    clear_dpre(d_h, r_h, nx, 2 * REACH, gh)
    for u in range(nu):
        for m in range(ny // 2):
            here = (u * ny // 2 + m) * LANES
            one, two = exchange_halves(vout[2 * m, u], vout[2 * m + 1, u], left2)
            o_ref[0, :, here : here + LANES] = one.astype(bf16)
            o_ref[1, :, here : here + LANES] = two.astype(bf16)
    for copy in back:
        copy.wait_recv()
    for r in range(rows):
        grad_h[:, r * 2 * s : (r + 1) * 2 * s] = got_v[r].astype(f32)
    sum_v.exchange()

    def third_pass(x, carry):
        grad = grad_h[x].reshape(shape_h)
        for index, shift in enumerate(SHIFTS):
            place = place_of(x, shift, nv, shape_h, start)
            p = pre_ref[index, x]
            keep = (place >= 0) & (place < x_all)
            blend = b_ref[0, index : index + 1]
            store_dpre(
                d_h, r_h, x + 2 * REACH, index, gh, keep, grad, blend, p, sigma_of(p)
            )
        return carry

    lax.fori_loop(0, nx, third_pass, 0)
    sum_v.gather()
    gather_dpre(d_h, s_ref, nx + 2 * REACH, nv, gh, start - REACH, x_all)
    stacked = s_ref[: (nx + 2 * REACH) * nvs]
    pack_grads(wide[...].reshape((nx + 2 * REACH) * nvs, LANES), stacked, r_h, payload, 0)
    sum_h.scatter()
    grads = jnp.dot(stacked, w_ref[0], preferred_element_type=f32)
    grads = grads.reshape(nx + 2 * REACH, nvs, LANES)
    rim_sent[0] = grads[:REACH].astype(bf16)
    rim_sent[1] = grads[nx + REACH :].astype(bf16)
    rims = [
        remote(rim_sent.at[0], rim_got.at[1], rim_sem, 0, (row, left_col)),
        remote(rim_sent.at[1], rim_got.at[0], rim_sem, 1, (row, right_col)),
    ]
    for copy in rims:
        copy.start()
    grad_h[...] += grads[REACH : REACH + nx]
    sum_h.exchange()
    factor = float(nu * ny * nv * x_all) ** (-0.5)
    sum_v.finish()
    unpack_grads(sum_ref, 1, shear_ref, gw_v_ref, gb_v_ref, factor)
    for copy in rims:
        copy.wait_recv()

    @pl.when(col > 0)
    def _():
        grad_h[:REACH] += rim_got[0].astype(f32)

    @pl.when(col < cols - 1)
    def _():
        grad_h[nx - REACH :] += rim_got[1].astype(f32)

    sum_h.gather()
    for m in range(nv // 2):
        one = grad_h[:, 2 * m * s : (2 * m + 1) * s]
        two = grad_h[:, (2 * m + 1) * s : (2 * m + 2) * s]
        low, high = exchange_halves(one, two, left)
        lanes = slice(m * LANES, (m + 1) * LANES)
        dhor_ref[:s, :, lanes] = jnp.swapaxes(low, 0, 1).astype(bf16)
        dhor_ref[s:, :, lanes] = jnp.swapaxes(high, 0, 1).astype(bf16)
    sum_h.finish()
    unpack_grads(sum_ref, 0, shear_ref, gw_h_ref, gb_h_ref, factor)
    for copy in halo + there + back + rims:
        copy.wait_send()


def hand_out_kernel(*refs):
    count = len(refs) // 2
    for source, target in zip(refs[:count], refs[count:]):
        target[...] = source[...]


def hand_out(*arrays):
    whole = pl.BlockSpec(memory_space=pltpu.VMEM)
    return pl.pallas_call(
        hand_out_kernel,
        out_shape=[jax.ShapeDtypeStruct(a.shape, a.dtype) for a in arrays],
        in_specs=[whole] * len(arrays),
        out_specs=[whole] * len(arrays),
        compiler_params=pltpu.CompilerParams(vmem_limit_bytes=VMEM_LIMIT),
        name="hand_out",
    )(*arrays)


def per_device(features, weight_h, weight_v, beta_h, beta_v, shear_set, cotangent):
    rows, cols = lax.axis_size("vrow"), lax.axis_size("img")
    channels = weight_h.shape[0]
    u_local, y_all, x_local, merged = features.shape
    v_all = merged // channels
    v_local = v_all // rows
    u_all = u_local * rows
    s_h = u_local * y_all // 2
    s_v = v_local * x_local // 2
    f32, bf16 = jnp.float32, jnp.bfloat16
    count = len(SHIFTS)
    assert u_local == 1 and v_local == 2 and s_h % 8 == 0 and s_v % 8 == 0

    def tap_major(weight):
        return jnp.transpose(weight, (2, 3, 0, 1)).reshape(9, channels, channels)

    flat_h = (x_local, v_all * s_h, LANES)
    flat_v = (y_all, u_all * s_v, LANES)
    four_v = (y_all, u_all, s_v, LANES)
    rim = (REACH, v_all * s_h, LANES)
    grads = 5 * channels
    chunk = (grads // cols, LANES)
    gh, gv = s_h // 8, s_v // 8
    wide_x, wide_y = x_local + 2 * REACH, y_all + 2 * REACH
    products = max(wide_x * (v_all + 2) * gh, wide_y * (u_all + 2) * gv)
    vmem, dma = pltpu.VMEM, pltpu.SemaphoreType.DMA
    whole = pl.BlockSpec(memory_space=vmem)
    shape = jax.ShapeDtypeStruct
    results = pl.pallas_call(
        functools.partial(field_kernel, rows, cols),
        out_shape=[
            shape(cotangent.shape, bf16),
            shape(features.shape[1:], bf16),
            shape((9, channels, channels), f32),
            shape((9, channels, channels), f32),
            shape(beta_h.shape, f32),
            shape(beta_v.shape, f32),
        ],
        in_specs=[whole] * 5 + [pl.BlockSpec(memory_space=pltpu.SMEM), whole],
        out_specs=[whole] * 6,
        scratch_shapes=[
            vmem((wide_x,) + flat_h[1:], bf16),
            vmem((2, 9 * LANES, LANES), bf16),
            vmem((2, 8, LANES), f32),
            vmem((9, products, 8, LANES), f32),
            vmem((count, x_local, v_all * gh, 8, LANES), f32),
            vmem((x_local, v_all, s_h, LANES), f32),
            vmem((rows - 1, y_all * s_v, LANES), bf16),
            vmem((rows, y_all * s_v, LANES), bf16),
            vmem(flat_v, bf16),
            vmem(four_v, f32),
            vmem(four_v, f32),
            vmem(four_v, f32),
            vmem((rows - 1, x_local, 2 * s_h, LANES), bf16),
            vmem((rows, x_local, 2 * s_h, LANES), bf16),
            vmem(flat_h, f32),
            vmem((2,) + rim, bf16),
            vmem((2,) + rim, bf16),
            vmem((2, grads, LANES), f32),
            vmem((2, grads, LANES), f32),
            vmem((2, cols - 1) + chunk, f32),
            vmem((2, rows) + chunk, f32),
            vmem((max(wide_x * flat_h[1], y_all * flat_v[1]), 9 * LANES), bf16),
            vmem((count, x_local + 4 * REACH, (v_all + 2) * gh, 8, LANES), f32),
            vmem((count, wide_y, (u_all + 2) * gv, 8, LANES), f32),
            vmem((count, 8, LANES), f32),
            vmem((count, 8, LANES), f32),
            dma((2, 2)),
            dma((2, rows - 1)),
            dma((2, rows - 1)),
            dma((2, 2)),
            dma((2, 2, cols - 1)),
            dma((2, 2, rows - 1)),
            dma((2, 2, cols - 1)),
        ],
        compiler_params=pltpu.CompilerParams(
            collective_id=0, has_side_effects=True, vmem_limit_bytes=VMEM_LIMIT
        ),
        name="light_field",
    )(
        features.reshape(features.shape[1:]),
        tap_major(weight_h),
        tap_major(weight_v),
        beta_h,
        beta_v,
        shear_set,
        cotangent,
    )

    output, dhor, gw_h, gw_v, gb_h, gb_v = hand_out(*results)

    def tap_minor(grad):
        return jnp.transpose(grad.reshape(3, 3, channels, channels), (2, 3, 0, 1))

    return output, dhor.reshape(features.shape), tap_minor(gw_h), tap_minor(gw_v), gb_h, gb_v


def solution(mesh):
    placed = (P("vrow", None, "img", None), P(), P(), P(), P(), P(), P("vrow", "img", None))
    return jax.shard_map(
        per_device,
        mesh=mesh,
        in_specs=placed,
        out_specs=(P("vrow", "img", None), P("vrow", None, "img", None), P(), P(), P(), P()),
        check_vma=False,
    )
```

```python
import functools

import jax
import jax.numpy as jnp
from jax import lax
from jax.experimental import pallas as pl
from jax.experimental.pallas import tpu as pltpu
from jax.sharding import PartitionSpec as P

SHIFTS = (-2, -1, 0, 1, 2)
REACH = 3
TAPS = tuple((i, j) for i in (-1, 0, 1) for j in (-1, 0, 1))
LANES = 128
MESH = pl.DeviceIdType.MESH
VMEM_LIMIT = 60 * 1024 * 1024


def place_of(x, shift, views, shape, start):
    view = lax.broadcasted_iota(jnp.int32, shape, 0) // (shape[0] // views) - views // 2
    return start + x - shift * view


def dot_t(x, y):
    return lax.dot_general(x, y, (((1,), (1,)), ((), ())), preferred_element_type=jnp.float32)


def tap_products(f_ref, w_ref, which, z_ref, views, first, length):
    rows = f_ref.shape[1]
    per = rows // 8
    step = per // views * (views + 2)
    source = f_ref[first : first + length].reshape(length * rows, LANES)
    for t in range(0, 9, 2):
        last = min(t + 2, 9)
        got = dot_t(source, w_ref[which, t * LANES : last * LANES])
        for k in range(t, last):
            part = got[:, (k - t) * LANES : (k - t + 1) * LANES]
            for x in range(length):
                here = (first + x) * step + per // views
                z_ref[k, here : here + per] = part[x * rows : (x + 1) * rows].reshape(
                    per, 8, LANES
                )


def clear_products(z_ref, columns, views, group, rim):
    step = (views + 2) * group
    side = jnp.zeros((9, group, 8, LANES), jnp.float32)

    def body(x, carry):
        z_ref[:, pl.ds(x * step, group)] = side
        z_ref[:, pl.ds(x * step + (views + 1) * group, group)] = side
        return carry

    lax.fori_loop(0, columns, body, 0)
    if rim:
        zero = jnp.zeros((9, rim * step, 8, LANES), jnp.float32)
        z_ref[:, : rim * step] = zero
        z_ref[:, (columns - rim) * step : columns * step] = zero


def preact_at(z_ref, x, views, group, shift, place, total):
    step = (views + 2) * group
    sums = {}
    for t, (i, j) in enumerate(TAPS):
        here = (x + (REACH + j + shift * i)) * step + (1 + i) * group
        term = z_ref[t, pl.ds(here, views * group)]
        sums[j] = term if j not in sums else sums[j] + term
    low = jnp.where(place != 0, sums[-1], 0.0)
    high = jnp.where(place != total - 1, sums[1], 0.0)
    return sums[0] + low + high


def sigma_of(p):
    return 0.5 * jnp.tanh(0.5 * p) + 0.5


def store_dpre(d_ref, r_ref, x, index, group, keep, grad, blend, p, sigma):
    act = jnp.where(keep, p * sigma, 0.0)
    r_ref[index] += jnp.sum(grad * act, axis=0)
    slope = sigma * (1.0 + p * (1.0 - sigma))
    dpre = jnp.where(keep, blend * grad * slope, 0.0)
    d_ref[index, x, group : group + grad.shape[0]] = dpre


def clear_dpre(d_ref, r_ref, nx, pad, group):
    count, _, per, _, _ = d_ref.shape
    r_ref[...] = jnp.zeros_like(r_ref)
    rim = jnp.zeros((count, pad, per, 8, LANES), jnp.float32)
    d_ref[:, 0:pad] = rim
    d_ref[:, pad + nx : 2 * pad + nx] = rim
    side = jnp.zeros((count, nx, group, 8, LANES), jnp.float32)
    d_ref[:, pad : pad + nx, 0:group] = side
    d_ref[:, pad : pad + nx, per - group : per] = side


def gather_dpre(d_ref, s_ref, length, views, group, start, total):
    per = views * group

    def body(x, carry):
        sums = [None] * 9
        for index, shift in enumerate(SHIFTS):
            place = place_of(x, shift, views, (per, 8, LANES), start)
            inside = (place >= 0) & (place < total)
            for t, (i, j) in enumerate(TAPS):
                term = d_ref[
                    index, x + (REACH - j - shift * i), (1 - i) * group : (1 - i) * group + per
                ]
                if j != 0:
                    term = jnp.where(inside, term, 0.0)
                sums[t] = term if sums[t] is None else sums[t] + term
        here = pl.ds(pl.multiple_of(x * (per * 8), 16), per * 8)
        for t in range(9):
            s_ref[here, t * LANES : (t + 1) * LANES] = (
                sums[t].reshape(per * 8, LANES).astype(jnp.bfloat16)
            )
        return carry

    lax.fori_loop(0, length, body, 0)


def pack_grads(source, stacked, r_ref, out_ref, which):
    wide = lax.dot_general(
        source, stacked, (((0,), (0,)), ((), ())), preferred_element_type=jnp.float32
    )
    half = LANES // 2
    first, second = wide[:half], wide[half:]
    left = lax.broadcasted_iota(jnp.int32, (half, LANES), 1) < half
    sums = jnp.sum(r_ref[...], axis=1)
    sums = sums + pltpu.roll(sums, half, 1)
    for m in range(5):
        low = slice(2 * m * LANES, (2 * m + 1) * LANES)
        even = first[:, low] + pltpu.roll(second[:, low], half, 1)
        if m < 4:
            high = slice((2 * m + 1) * LANES, (2 * m + 2) * LANES)
            odd = pltpu.roll(first[:, high], half, 1) + second[:, high]
        else:
            odd = jnp.concatenate(
                [sums, jnp.zeros((half - sums.shape[0], LANES), jnp.float32)], axis=0
            )
        out_ref[which, m * half : (m + 1) * half] = jnp.where(left, even, odd)


def exchange_halves(one, two, left):
    return jnp.where(left, one, half_roll(two)), jnp.where(left, half_roll(one), two)


def stack_weights(weight_ref, w_ref, which, left):
    half = LANES // 2
    for t in range(9):
        tap = weight_ref[t].astype(jnp.float32)
        twice = jnp.concatenate([tap, tap], axis=1)
        both = jnp.concatenate(
            [jnp.where(left, twice, 0.0), jnp.where(left, 0.0, twice)], axis=0
        )
        w_ref[which, t * LANES : (t + 1) * LANES] = both.astype(jnp.bfloat16)


def stack_blends(beta_ref, shear_ref, b_ref, which):
    beta = beta_ref[...]
    beta = jnp.concatenate([beta, beta], axis=1)
    for index, shift in enumerate(SHIFTS):
        total = jnp.zeros((1, LANES), jnp.float32)
        for k in range(beta.shape[0]):
            total = total + jnp.where(shear_ref[k] == shift, 1.0, 0.0) * beta[k : k + 1]
        b_ref[which, index : index + 1] = total


def unpack_grads(sum_ref, which, shear_ref, weight_ref, beta_ref, factor):
    half = LANES // 2
    for m in range(5):
        tile = sum_ref[which, m * half : (m + 1) * half] * factor
        turned = jnp.transpose(tile)
        weight_ref[2 * m] = turned[:half]
        if m < 4:
            weight_ref[2 * m + 1] = turned[half:]
        else:
            raw = half_roll(tile[:8])[:, :half]
    for k in range(beta_ref.shape[0]):
        total = jnp.zeros((1, half), jnp.float32)
        for index, shift in enumerate(SHIFTS):
            total = total + jnp.where(shear_ref[k] == shift, 1.0, 0.0) * raw[index : index + 1]
        beta_ref[k : k + 1] = total


def half_roll(x):
    return pltpu.roll(x, LANES // 2, x.ndim - 1)


def remote(src, dst, sems, k, device):
    return pltpu.make_async_remote_copy(
        src_ref=src,
        dst_ref=dst,
        send_sem=sems.at[0, k],
        recv_sem=sems.at[1, k],
        device_id=device,
        device_id_type=MESH,
    )


class Sum:
    def __init__(self, rows, cols, x_ref, o_ref, heard, totals, sem_a, sem_b, sem_c):
        self.rows, self.cols = rows, cols
        self.x_ref, self.o_ref, self.heard, self.totals = x_ref, o_ref, heard, totals
        self.sems = (sem_a, sem_b, sem_c)
        self.row, self.col = lax.axis_index("vrow"), lax.axis_index("img")
        self.size = heard.shape[1]
        self.sent = []

    def chunk(self, index):
        return pl.ds(pl.multiple_of(index * self.size, 8), self.size)

    def scatter(self):
        self.first = []
        for k in range(1, self.cols):
            to = lax.rem(self.col + k, self.cols)
            source = self.x_ref.at[self.chunk(to)]
            copy = remote(source, self.heard.at[k - 1], self.sems[0], k - 1, (self.row, to))
            copy.start()
            self.first.append(copy)

    def exchange(self):
        total = self.x_ref[self.chunk(self.col)]
        for k, copy in enumerate(self.first):
            copy.wait_recv()
            total = total + self.heard[k]
        self.totals[self.row] = total
        self.second = []
        for k in range(1, self.rows):
            to = lax.rem(self.row + k, self.rows)
            mine = self.totals.at[self.row]
            copy = remote(mine, mine, self.sems[1], k - 1, (to, self.col))
            copy.start()
            self.second.append(copy)

    def gather(self):
        for copy in self.second:
            copy.wait_recv()
        total = self.totals[0]
        for k in range(1, self.rows):
            total = total + self.totals[k]
        self.o_ref[self.chunk(self.col)] = total
        self.third = []
        for k in range(1, self.cols):
            to = lax.rem(self.col + k, self.cols)
            mine = self.o_ref.at[self.chunk(self.col)]
            copy = remote(mine, mine, self.sems[2], k - 1, (self.row, to))
            copy.start()
            self.third.append(copy)

    def finish(self):
        for copy in self.third:
            copy.wait_recv()
        for copy in self.first + self.second + self.third:
            copy.wait_send()


def field_kernel(
    rows,
    cols,
    f_ref,
    weight_h_ref,
    weight_v_ref,
    beta_h_ref,
    beta_v_ref,
    shear_ref,
    c_ref,
    o_ref,
    dhor_ref,
    gw_h_ref,
    gw_v_ref,
    gb_h_ref,
    gb_v_ref,
    wide,
    w_ref,
    b_ref,
    z_ref,
    pre_ref,
    hfeat,
    send_h,
    got_h,
    vert,
    cot,
    vout,
    dvert,
    send_v,
    got_v,
    grad_h,
    rim_sent,
    rim_got,
    payload,
    sum_ref,
    heard,
    totals,
    s_ref,
    d_h,
    d_v,
    r_h,
    r_v,
    halo_sem,
    there_sem,
    back_sem,
    rim_sem,
    sum_a,
    sum_b,
    sum_c,
):
    row, col = lax.axis_index("vrow"), lax.axis_index("img")
    nx, nvs, _ = grad_h.shape
    ny, nu, sv, _ = dvert.shape
    s = f_ref.shape[0] // 2
    nv = nvs // s
    gh, gv = s // 8, sv // 8
    x_all = nx * cols
    start = col * nx
    f32, bf16 = jnp.float32, jnp.bfloat16
    shape_h, shape_v = (nv * gh, 8, LANES), (nu * gv, 8, LANES)
    left = lax.broadcasted_iota(jnp.int32, (1, 1, LANES), 2) < LANES // 2
    left2 = lax.broadcasted_iota(jnp.int32, (1, LANES), 1) < LANES // 2
    right_col, left_col = lax.rem(col + 1, cols), lax.rem(col + cols - 1, cols)

    barrier = pltpu.get_barrier_semaphore()
    for k in range(1, cols):
        peer = (row, lax.rem(col + k, cols))
        pl.semaphore_signal(barrier, inc=1, device_id=peer, device_id_type=MESH)
    for k in range(1, rows):
        peer = (lax.rem(row + k, rows), col)
        pl.semaphore_signal(barrier, inc=1, device_id=peer, device_id_type=MESH)

    for m in range(nv // 2):
        block = f_ref[:, :, m * LANES : (m + 1) * LANES].astype(f32)
        low, high = jnp.swapaxes(block[:s], 0, 1), jnp.swapaxes(block[s:], 0, 1)
        both = jnp.concatenate(exchange_halves(low, high, left), axis=1)
        wide[REACH : REACH + nx, m * 2 * s : (m + 1) * 2 * s] = both.astype(bf16)
    pl.semaphore_wait(barrier, cols + rows - 2)

    halo = [
        remote(
            wide.at[pl.ds(nx, REACH)],
            wide.at[pl.ds(0, REACH)],
            halo_sem,
            0,
            (row, right_col),
        ),
        remote(
            wide.at[pl.ds(REACH, REACH)],
            wide.at[pl.ds(nx + REACH, REACH)],
            halo_sem,
            1,
            (row, left_col),
        ),
    ]
    for copy in halo:
        copy.start()
    stack_weights(weight_h_ref, w_ref, 0, left2)
    stack_blends(beta_h_ref, shear_ref, b_ref, 0)
    clear_products(z_ref, nx + 2 * REACH, nv, gh, 0)
    tap_products(wide, w_ref, 0, z_ref, nv, REACH, nx)
    for copy in halo:
        copy.wait_recv()

    @pl.when(col == 0)
    def _():
        wide[:REACH] = jnp.zeros((REACH, nvs, LANES), bf16)

    @pl.when(col == cols - 1)
    def _():
        wide[nx + REACH :] = jnp.zeros((REACH, nvs, LANES), bf16)

    tap_products(wide, w_ref, 0, z_ref, nv, 0, REACH)
    tap_products(wide, w_ref, 0, z_ref, nv, nx + REACH, REACH)

    def first_pass(x, carry):
        out = wide[x + REACH].astype(f32).reshape(shape_h)
        for index, shift in enumerate(SHIFTS):
            place = place_of(x, shift, nv, shape_h, start)
            p = preact_at(z_ref, x, nv, gh, shift, place, x_all)
            pre_ref[index, x] = p
            keep = (place >= 0) & (place < x_all)
            out = out + b_ref[0, index : index + 1] * jnp.where(keep, p * sigma_of(p), 0.0)
        hfeat[x] = out.reshape(nv, s, LANES)
        return carry

    lax.fori_loop(0, nx, first_pass, 0)

    def block_there(to):
        views = hfeat[:, pl.ds(2 * to, 2)]
        low, high = exchange_halves(views[:, 0], views[:, 1], left)
        both = [jnp.swapaxes(low, 0, 1), jnp.swapaxes(high, 0, 1)]
        return jnp.concatenate(both, axis=0).reshape(ny * sv, LANES).astype(bf16)

    there = []
    for k in range(1, rows):
        to = lax.rem(row + k, rows)
        send_h[k - 1] = block_there(to)
        copy = remote(send_h.at[k - 1], got_h.at[row], there_sem, k - 1, (to, col))
        copy.start()
        there.append(copy)
    got_h[row] = block_there(row)

    sum_h, sum_v = [
        Sum(
            rows,
            cols,
            payload.at[n],
            sum_ref.at[n],
            heard.at[n],
            totals.at[n],
            sum_a.at[n],
            sum_b.at[n],
            sum_c.at[n],
        )
        for n in range(2)
    ]
    stack_weights(weight_v_ref, w_ref, 1, left2)
    stack_blends(beta_v_ref, shear_ref, b_ref, 1)
    clear_products(z_ref, ny + 2 * REACH, nu, gv, REACH)
    clear_dpre(d_v, r_v, ny, REACH, gv)
    for u in range(nu):
        for m in range(ny // 2):
            here = (u * ny // 2 + m) * LANES
            one = c_ref[0, :, here : here + LANES].astype(f32)
            two = c_ref[1, :, here : here + LANES].astype(f32)
            cot[2 * m, u], cot[2 * m + 1, u] = exchange_halves(one, two, left2)
    for copy in there:
        copy.wait_recv()
    parts = [got_h[u].astype(f32).reshape(ny, 1, sv, LANES) for u in range(rows)]
    vert[...] = jnp.concatenate(parts, axis=1).reshape(ny, nu * sv, LANES).astype(bf16)

    for t in range(0, 9, 2):
        last = min(t + 2, 9)
        got = dot_t(vert[...].reshape(ny * nu * sv, LANES), w_ref[1, t * LANES : last * LANES])
        for k in range(t, last):
            part = got[:, (k - t) * LANES : (k - t + 1) * LANES]
            for y in range(ny):
                here = (REACH + y) * (nu + 2) * gv + gv
                z_ref[k, here : here + nu * gv] = part[y * nu * sv : (y + 1) * nu * sv].reshape(
                    shape_v
                )

    def second_pass(y, carry):
        out = vert[y].astype(f32).reshape(shape_v)
        grad = cot[y].reshape(shape_v)
        for index, shift in enumerate(SHIFTS):
            place = place_of(y, shift, nu, shape_v, 0)
            p = preact_at(z_ref, y, nu, gv, shift, place, ny)
            sigma = sigma_of(p)
            keep = (place >= 0) & (place < ny)
            blend = b_ref[1, index : index + 1]
            out = out + blend * jnp.where(keep, p * sigma, 0.0)
            store_dpre(d_v, r_v, y + REACH, index, gv, keep, grad, blend, p, sigma)
        vout[y] = out.reshape(nu, sv, LANES)
        return carry

    lax.fori_loop(0, ny, second_pass, 0)
    gather_dpre(d_v, s_ref, ny, nu, gv, 0, ny)
    stacked = s_ref[: ny * nu * sv]
    grads = jnp.dot(stacked, w_ref[1], preferred_element_type=f32)
    dvert[...] = cot[...] + grads.reshape(dvert.shape)

    def block_back(to):
        block = dvert[:, pl.ds(to, 1)].reshape(ny, sv, LANES)
        low, high = jnp.swapaxes(block[:s], 0, 1), jnp.swapaxes(block[s:], 0, 1)
        both = jnp.concatenate(exchange_halves(low, high, left), axis=1)
        return both.astype(bf16)

    back = []
    for k in range(1, rows):
        to = lax.rem(row + k, rows)
        send_v[k - 1] = block_back(to)
        copy = remote(send_v.at[k - 1], got_v.at[row], back_sem, k - 1, (to, col))
        copy.start()
        back.append(copy)
    got_v[row] = block_back(row)
    pack_grads(vert[...].reshape(ny * nu * sv, LANES), stacked, r_v, payload, 1)
    sum_v.scatter()
    clear_dpre(d_h, r_h, nx, 2 * REACH, gh)
    for u in range(nu):
        for m in range(ny // 2):
            here = (u * ny // 2 + m) * LANES
            one, two = exchange_halves(vout[2 * m, u], vout[2 * m + 1, u], left2)
            o_ref[0, :, here : here + LANES] = one.astype(bf16)
            o_ref[1, :, here : here + LANES] = two.astype(bf16)
    for copy in back:
        copy.wait_recv()
    for r in range(rows):
        grad_h[:, r * 2 * s : (r + 1) * 2 * s] = got_v[r].astype(f32)

    def third_pass(x, carry):
        grad = grad_h[x].reshape(shape_h)
        for index, shift in enumerate(SHIFTS):
            place = place_of(x, shift, nv, shape_h, start)
            p = pre_ref[index, x]
            keep = (place >= 0) & (place < x_all)
            blend = b_ref[0, index : index + 1]
            store_dpre(
                d_h, r_h, x + 2 * REACH, index, gh, keep, grad, blend, p, sigma_of(p)
            )
        return carry

    lax.fori_loop(0, nx, third_pass, 0)
    sum_v.exchange()
    gather_dpre(d_h, s_ref, nx + 2 * REACH, nv, gh, start - REACH, x_all)
    stacked = s_ref[: (nx + 2 * REACH) * nvs]
    pack_grads(wide[...].reshape((nx + 2 * REACH) * nvs, LANES), stacked, r_h, payload, 0)
    sum_h.scatter()
    sum_v.gather()
    grads = jnp.dot(stacked, w_ref[0], preferred_element_type=f32)
    grads = grads.reshape(nx + 2 * REACH, nvs, LANES)
    rim_sent[0] = grads[:REACH].astype(bf16)
    rim_sent[1] = grads[nx + REACH :].astype(bf16)
    rims = [
        remote(rim_sent.at[0], rim_got.at[1], rim_sem, 0, (row, left_col)),
        remote(rim_sent.at[1], rim_got.at[0], rim_sem, 1, (row, right_col)),
    ]
    for copy in rims:
        copy.start()
    grad_h[...] += grads[REACH : REACH + nx]
    sum_h.exchange()
    for copy in rims:
        copy.wait_recv()

    @pl.when(col > 0)
    def _():
        grad_h[:REACH] += rim_got[0].astype(f32)

    @pl.when(col < cols - 1)
    def _():
        grad_h[nx - REACH :] += rim_got[1].astype(f32)

    sum_h.gather()
    for m in range(nv // 2):
        one = grad_h[:, 2 * m * s : (2 * m + 1) * s]
        two = grad_h[:, (2 * m + 1) * s : (2 * m + 2) * s]
        low, high = exchange_halves(one, two, left)
        lanes = slice(m * LANES, (m + 1) * LANES)
        dhor_ref[:s, :, lanes] = jnp.swapaxes(low, 0, 1).astype(bf16)
        dhor_ref[s:, :, lanes] = jnp.swapaxes(high, 0, 1).astype(bf16)
    factor = float(nu * ny * nv * x_all) ** (-0.5)
    sum_v.finish()
    unpack_grads(sum_ref, 1, shear_ref, gw_v_ref, gb_v_ref, factor)
    sum_h.finish()
    unpack_grads(sum_ref, 0, shear_ref, gw_h_ref, gb_h_ref, factor)
    for copy in halo + there + back + rims:
        copy.wait_send()


def hand_out_kernel(*refs):
    count = len(refs) // 2
    for source, target in zip(refs[:count], refs[count:]):
        target[...] = source[...]


def hand_out(*arrays):
    whole = pl.BlockSpec(memory_space=pltpu.VMEM)
    return pl.pallas_call(
        hand_out_kernel,
        out_shape=[jax.ShapeDtypeStruct(a.shape, a.dtype) for a in arrays],
        in_specs=[whole] * len(arrays),
        out_specs=[whole] * len(arrays),
        compiler_params=pltpu.CompilerParams(vmem_limit_bytes=VMEM_LIMIT),
        name="hand_out",
    )(*arrays)


def per_device(features, weight_h, weight_v, beta_h, beta_v, shear_set, cotangent):
    rows, cols = lax.axis_size("vrow"), lax.axis_size("img")
    channels = weight_h.shape[0]
    u_local, y_all, x_local, merged = features.shape
    v_all = merged // channels
    v_local = v_all // rows
    u_all = u_local * rows
    s_h = u_local * y_all // 2
    s_v = v_local * x_local // 2
    f32, bf16 = jnp.float32, jnp.bfloat16
    count = len(SHIFTS)
    assert u_local == 1 and v_local == 2 and s_h % 8 == 0 and s_v % 8 == 0

    def tap_major(weight):
        return jnp.transpose(weight, (2, 3, 0, 1)).reshape(9, channels, channels)

    flat_h = (x_local, v_all * s_h, LANES)
    flat_v = (y_all, u_all * s_v, LANES)
    four_v = (y_all, u_all, s_v, LANES)
    rim = (REACH, v_all * s_h, LANES)
    grads = 5 * channels
    chunk = (grads // cols, LANES)
    gh, gv = s_h // 8, s_v // 8
    wide_x, wide_y = x_local + 2 * REACH, y_all + 2 * REACH
    products = max(wide_x * (v_all + 2) * gh, wide_y * (u_all + 2) * gv)
    vmem, dma = pltpu.VMEM, pltpu.SemaphoreType.DMA
    whole = pl.BlockSpec(memory_space=vmem)
    shape = jax.ShapeDtypeStruct
    results = pl.pallas_call(
        functools.partial(field_kernel, rows, cols),
        out_shape=[
            shape(cotangent.shape, bf16),
            shape(features.shape[1:], bf16),
            shape((9, channels, channels), f32),
            shape((9, channels, channels), f32),
            shape(beta_h.shape, f32),
            shape(beta_v.shape, f32),
        ],
        in_specs=[whole] * 5 + [pl.BlockSpec(memory_space=pltpu.SMEM), whole],
        out_specs=[whole] * 6,
        scratch_shapes=[
            vmem((wide_x,) + flat_h[1:], bf16),
            vmem((2, 9 * LANES, LANES), bf16),
            vmem((2, 8, LANES), f32),
            vmem((9, products, 8, LANES), f32),
            vmem((count, x_local, v_all * gh, 8, LANES), f32),
            vmem((x_local, v_all, s_h, LANES), f32),
            vmem((rows - 1, y_all * s_v, LANES), bf16),
            vmem((rows, y_all * s_v, LANES), bf16),
            vmem(flat_v, bf16),
            vmem(four_v, f32),
            vmem(four_v, f32),
            vmem(four_v, f32),
            vmem((rows - 1, x_local, 2 * s_h, LANES), bf16),
            vmem((rows, x_local, 2 * s_h, LANES), bf16),
            vmem(flat_h, f32),
            vmem((2,) + rim, bf16),
            vmem((2,) + rim, bf16),
            vmem((2, grads, LANES), f32),
            vmem((2, grads, LANES), f32),
            vmem((2, cols - 1) + chunk, f32),
            vmem((2, rows) + chunk, f32),
            vmem((max(wide_x * flat_h[1], y_all * flat_v[1]), 9 * LANES), bf16),
            vmem((count, x_local + 4 * REACH, (v_all + 2) * gh, 8, LANES), f32),
            vmem((count, wide_y, (u_all + 2) * gv, 8, LANES), f32),
            vmem((count, 8, LANES), f32),
            vmem((count, 8, LANES), f32),
            dma((2, 2)),
            dma((2, rows - 1)),
            dma((2, rows - 1)),
            dma((2, 2)),
            dma((2, 2, cols - 1)),
            dma((2, 2, rows - 1)),
            dma((2, 2, cols - 1)),
        ],
        compiler_params=pltpu.CompilerParams(
            collective_id=0, has_side_effects=True, vmem_limit_bytes=VMEM_LIMIT
        ),
        name="light_field",
    )(
        features.reshape(features.shape[1:]),
        tap_major(weight_h),
        tap_major(weight_v),
        beta_h,
        beta_v,
        shear_set,
        cotangent,
    )

    output, dhor, gw_h, gw_v, gb_h, gb_v = hand_out(*results)

    def tap_minor(grad):
        return jnp.transpose(grad.reshape(3, 3, channels, channels), (2, 3, 0, 1))

    return output, dhor.reshape(features.shape), tap_minor(gw_h), tap_minor(gw_v), gb_h, gb_v


def solution(mesh):
    placed = (P("vrow", None, "img", None), P(), P(), P(), P(), P(), P("vrow", "img", None))
    return jax.shard_map(
        per_device,
        mesh=mesh,
        in_specs=placed,
        out_specs=(P("vrow", "img", None), P("vrow", None, "img", None), P(), P(), P(), P()),
        check_vma=False,
    )
```
